32 devices in a mesh: dom: 8 (over z, x), rep: 4 (over y, core).
Axes of the slice: x: 2, y: 2, z: 4, core: 2. Of those that a mesh axis runs over, the one named last changes fastest.
Arguments:
- embeddings: float32 [262144, 256], P(('dom', 'rep')), may hold values from -1.5 to 1.5
- row_state: float32 [262144], P(('dom', 'rep')), may hold values from 0.01 to 0.1
- relations: float32 [64, 256], replicated, may hold values from 0.1 to 1.9
- rel_state: float32 [64, 256], replicated, may hold values from 2 to 40
- edge_src: int32 [8, 4, 2, 4, 1000], P('dom', 'rep'), may hold values from 0 to 8191
- edge_dst: int32 [8, 4, 2, 4, 1000], P('dom', 'rep'), may hold values from 0 to 8191
- edge_rel: int32 [8, 4, 2, 4, 1000], P('dom', 'rep'), may hold values from 0 to 63
- batch_count: int32 [8, 4, 2], P('dom', 'rep'), may hold values from 1 to 4, as said below
Outputs:
- new_embeddings: float32 [262144, 256], P(('dom', 'rep'))
- new_row_state: float32 [262144], P(('dom', 'rep'))
- new_relations: float32 [64, 256], replicated
- new_rel_state: float32 [64, 256], replicated
The draws below stay inside these ranges and needn't reach their ends.
Inputs may be any that keep to these rules, and one draw needn't show every extreme that they name: `batch_count`: batches at or past the count are ignored; some bucket of each round set reaches 4.
All inputs are finite; a program needn't handle non-finite values.
Results may differ from the reference program's by a relative error of at most 0.0031.
Values may be sent and summed in bfloat16 or wider, within the bound.
No kernel may reach another device: no remote copies, remote signals or barrier semaphores. Data moves between devices by JAX's collectives and lax.ppermute only.
A program may use at most 128 MiB of HBM per device.

```python
import math
import jax
import jax.numpy as jnp
import numpy as np
from jax import lax

D = 256
REL = 64
ROWS_DEV = 8192
BATCH = 1000
NB_CAP = 4
ROUNDS = 2
NODES = 262144
N_DOM = 8
N_REP = 4


def draw_batch_count(key, part):
    key_extra = jax.random.fold_in(key, 11)
    key_keep = jax.random.fold_in(key, 12)
    key_place = jax.random.fold_in(key, 13)
    extra = jax.random.randint(key_extra, (N_DOM, N_REP, ROUNDS), 0, NB_CAP)
    keep_flag = jax.random.randint(key_keep, (N_DOM, N_REP, ROUNDS), 0, 2)
    counted = 1 + extra * keep_flag
    places = jax.random.randint(key_place, (ROUNDS,), 0, N_DOM * N_REP)
    flat_index = jnp.arange(N_DOM * N_REP, dtype=jnp.int32).reshape(N_DOM, N_REP, 1)
    counted = jnp.where(flat_index == places[None, None, :], NB_CAP, counted)
    return counted.astype(jnp.int32)


def touch_ends(values, own_key, least, largest):
    index_at = [jax.random.randint(jax.random.fold_in(own_key, axis), (), 0, length) for axis, length in enumerate(values.shape)]
    main_axis = values.shape.index(max(values.shape))
    next_to = index_at[:main_axis] + [(index_at[main_axis] + 1) % values.shape[main_axis]] + index_at[main_axis + 1:]
    return values.at[tuple(index_at)].set(least).at[tuple(next_to)].set(largest)


def steps_of(own_key, dims, pieces, least, top_value):
    def one(dim, parts):
        heights = jax.random.uniform(jax.random.fold_in(jax.random.fold_in(own_key, 6), dim), (parts,), jnp.float32, least / len(pieces), top_value / len(pieces))
        return jnp.repeat(jnp.exp(heights), dims[dim] // parts).reshape((-1,) + (1,) * (len(dims) - dim - 1))

    level = one(*pieces[0])
    for cut in pieces[1:]:
        level = level * one(*cut)
    return level


def rank_bounds(count, skew):
    portions = [(1 << 20) // math.isqrt(rank ** skew) + 1 for rank in range(1, count + 1)]
    deviation = 1 + sum(portions) // (1 << 30)
    return np.cumsum(np.array([max(1, weight // deviation) for weight in portions]))


def skewed_ids(key, shape, count, lean):
    table = rank_bounds(count, lean)
    pick = jax.random.randint(jax.random.fold_in(key, 1), shape, 0, int(table[count - 1]))
    grade = jnp.searchsorted(jnp.asarray(table, jnp.int32), pick, side="right")
    return jax.random.permutation(jax.random.fold_in(key, 2), count)[grade].astype(jnp.int32)


def centred(key, extent, deviation, most, pieces=(), kind=jnp.bfloat16):
    values = deviation * jax.random.normal(key, extent, jnp.float32)
    if pieces:
        values = values * steps_of(key, extent, pieces, -0.22, 0.18)
    return jnp.clip(values, -most, most).astype(kind)


def setup_inputs(seed: int = 0) -> dict:
    keys = jax.random.split(jax.random.key(seed), 9)
    embeddings = centred(keys[0], (NODES, D), 0.25, 1.5, ((0, 32),), jnp.float32)
    row_state = jnp.clip(jnp.exp(math.log(0.1) - 2.3025851 * jax.random.uniform(keys[1], (NODES,), jnp.float32) ** steps_of(keys[1], (NODES,), ((0, 32),), -0.2, 0.2)), 0.01, 0.1)
    relations = jnp.clip(1.0 + 0.18 * jax.random.normal(keys[2], (REL, D), jnp.float32), 0.1, 1.9)
    rel_state = jnp.clip(jnp.exp(jax.random.uniform(keys[3], (REL, D), jnp.float32, math.log(2.0), math.log(40.0))), 2.0, 40.0)
    edge_src = touch_ends(jax.random.randint(keys[4], (N_DOM, N_REP, ROUNDS, NB_CAP, BATCH), 0, ROWS_DEV), jax.random.fold_in(keys[4], 1), 0, ROWS_DEV - 1).astype(jnp.int32)
    edge_dst = touch_ends(jax.random.randint(keys[5], (N_DOM, N_REP, ROUNDS, NB_CAP, BATCH), 0, ROWS_DEV), jax.random.fold_in(keys[5], 1), 0, ROWS_DEV - 1).astype(jnp.int32)
    edge_rel = touch_ends(skewed_ids(keys[6], (N_DOM, N_REP, ROUNDS, NB_CAP, BATCH), REL, 2), jax.random.fold_in(keys[6], 3), 0, REL - 1).astype(jnp.int32)
    batch_count = draw_batch_count(jax.random.fold_in(keys[8], 71), 0)
    return dict(embeddings=embeddings, row_state=row_state, relations=relations, rel_state=rel_state, edge_src=edge_src, edge_dst=edge_dst, edge_rel=edge_rel, batch_count=batch_count)


learn_rate = 0.1
rel_rate = 0.1

def batch_terms(source_rows, target_rows, kind_index, relations):
    rel_count = relations.shape[0]
    onehot = (kind_index[:, None] == jnp.arange(rel_count, dtype=jnp.int32)[None, :]).astype(relations.dtype)
    diagonal = jnp.dot(onehot, relations, precision=lax.Precision.HIGHEST)
    source_full = source_rows.astype(relations.dtype)
    queries = (source_full * diagonal).astype(jnp.bfloat16)
    scores = lax.dot_general(queries, target_rows, (((1,), (1,)), ((), ())), preferred_element_type=jnp.float32)
    size_rows = scores.shape[0]
    on_diag = jnp.arange(size_rows)[:, None] == jnp.arange(size_rows)[None, :]
    probs = jax.nn.sigmoid(scores)
    weights_bf = jnp.where(on_diag, probs - 1.0, probs / (size_rows - 1)).astype(jnp.bfloat16)
    grad_query = jnp.dot(weights_bf, target_rows, preferred_element_type=jnp.float32)
    grad_target = lax.dot_general(weights_bf, queries, (((0,), (0,)), ((), ())), preferred_element_type=jnp.float32)
    grad_source = grad_query * diagonal
    grad_rel = lax.dot_general(onehot, grad_query * source_full, (((0,), (0,)), ((), ())), precision=lax.Precision.HIGHEST)
    return (grad_source, grad_target, grad_rel)

def reference(embeddings, row_state, relations, rel_state, edge_src, edge_dst, edge_rel, batch_count):
    groups = N_DOM * N_REP
    bit_count = N_DOM.bit_length() - 1
    embed_table = embeddings.reshape(groups, ROWS_DEV, D)
    states = row_state.reshape(groups, ROWS_DEV)
    for number in range(ROUNDS):
        mask_value = 1 << bit_count - 1 - number
        rows_bf = embed_table.astype(jnp.bfloat16)

        def device_step(device, carried):
            row_grads, rel_grad = carried
            dom_index = device // N_REP
            rep_index = device % N_REP
            partner = (dom_index ^ mask_value) * N_REP + rep_index
            own_rows = rows_bf[device]
            other_rows = rows_bf[partner]
            live_batches = batch_count[dom_index, rep_index, number]

            def batch_step(batch_number, inner_carry):
                own_grad, other_grad, rel_inner = inner_carry
                sources = edge_src[dom_index, rep_index, number, batch_number]
                targets = edge_dst[dom_index, rep_index, number, batch_number]
                kind_index = edge_rel[dom_index, rep_index, number, batch_number]
                source_grad, target_grad, kind_grad = batch_terms(jnp.take(own_rows, sources, axis=0), jnp.take(other_rows, targets, axis=0), kind_index, relations)
                return (own_grad.at[sources].add(source_grad), other_grad.at[targets].add(target_grad), rel_inner + kind_grad)
            empty_grad = jnp.zeros((ROWS_DEV, D), embed_table.dtype)
            own_grad, other_grad, rel_grad = lax.fori_loop(0, live_batches, batch_step, (empty_grad, empty_grad, rel_grad))
            row_grads = row_grads.at[device].add(own_grad).at[partner].add(other_grad)
            return (row_grads, rel_grad)
        row_grads, rel_grad = lax.fori_loop(0, groups, device_step, (jnp.zeros_like(embed_table), jnp.zeros_like(relations)))
        states = states + lax.optimization_barrier(jnp.mean(row_grads * row_grads, axis=-1))
        embed_table = embed_table - learn_rate * row_grads / jnp.sqrt(states)[:, :, None]
        rel_state = rel_state + rel_grad * rel_grad
        relations = relations - rel_rate * rel_grad / jnp.sqrt(rel_state)
    return (embed_table.reshape(NODES, D), states.reshape(NODES), relations, rel_state)
```

```python
import functools

import jax
import jax.numpy as jnp
from jax import lax
from jax.experimental import pallas as pl
from jax.experimental.pallas import tpu as pltpu
from jax.sharding import PartitionSpec as P

ROUNDS = 2


learn_rate = 0.1
rel_rate = 0.1

f32 = jnp.float32
bf16 = jnp.bfloat16
MIB = 1 << 20
LANES = 128
SMEM_SPEC = pl.BlockSpec(memory_space=pltpu.SMEM)
VMEM_SPEC = pl.BlockSpec(memory_space=pltpu.VMEM)
ANY_SPEC = pl.BlockSpec(memory_space=pl.ANY)


def from_partner(shard, axis, distance):
    return lax.ppermute(shard, axis, [(i, i ^ distance) for i in range(lax.axis_size(axis))])


def sum_over(values, axis, largest=3):
    bits = lax.axis_size(axis).bit_length() - 1
    low = 0
    while low < bits:
        take = min(largest, bits - low)
        parts = [values] + [from_partner(values, axis, k << low) for k in range(1, 1 << take)]
        while len(parts) > 1:
            parts = [parts[i] + parts[i + 1] for i in range(0, len(parts), 2)]
        values = parts[0]
        low += take
    return values


def unroll_of(count):
    return max(d for d in range(1, 41) if count % d == 0)


def share(meta_ref):
    a, b = meta_ref[0], meta_ref[1]
    each = (a + b + 1) // 2
    return a, b, each


def send_slots(meta_ref):
    a, b, each = share(meta_ref)
    return jnp.minimum(a, each) + jnp.maximum(b - each, 0)


def own_slots(meta_ref):
    a, b, each = share(meta_ref)
    return jnp.minimum(b, each) + jnp.maximum(a - each, 0)


def send_base(meta_ref, slot, slots, batch):
    a, b, each = share(meta_ref)
    return jnp.where(slot < a, slot, slots + each + slot - a) * batch


def own_base(meta_ref, slot, slots, batch):
    a, b, each = share(meta_ref)
    return jnp.where(slot < b, slots + slot, each + slot - b) * batch


def load_table(rows_ref, table, sems):
    return [
        pltpu.make_async_copy(rows_ref.at[:, pl.ds(h * LANES, LANES)], table.at[h], sems.at[h])
        for h in range(table.shape[0])
    ]


def gather_rows(index_ref, base, batch, table, buffer, out_ref):
    unroll = unroll_of(batch)

    def step(i, carry):
        at = i * unroll
        for u in range(unroll):
            row = index_ref[base + at + u]
            for h in range(table.shape[0]):
                buffer[h, pl.ds(at + u, 1), :] = table[h, pl.ds(row, 1), :]
        return carry

    lax.fori_loop(0, batch // unroll, step, 0)
    for h in range(table.shape[0]):
        out_ref[:, h * LANES : (h + 1) * LANES] = buffer[h].astype(bf16)


def clear_tail(buffer, batch):
    if buffer.shape[1] > batch:
        buffer[:, batch:, :] = jnp.zeros((buffer.shape[0], buffer.shape[1] - batch, LANES), f32)


def scatter_rows(index_ref, base, batch, grads, totals):
    unroll = unroll_of(batch)

    def step(i, carry):
        at = i * unroll
        for u in range(unroll):
            row = index_ref[base + at + u]
            total = totals[u % len(totals)]
            for h in range(total.shape[0]):
                total[h, pl.ds(row, 1), :] += grads[h, pl.ds(at + u, 1), :]
        return carry

    lax.fori_loop(0, batch // unroll, step, 0)


def first_gather(batch, index_ref, rows_ref, sent_ref, table, buffer, sems):
    copies = load_table(rows_ref, table, sems)
    for copy in copies:
        copy.start()
    clear_tail(buffer, batch)
    for copy in copies:
        copy.wait()
    gather_rows(index_ref, 0, batch, table, buffer, sent_ref)


def other_gathers(batch, slots, meta_ref, index_ref, rows_ref, *refs):
    outs, (table, buffer, sems) = refs[:-3], refs[-3:]
    copies = load_table(rows_ref, table, sems)
    for copy in copies:
        copy.start()
    clear_tail(buffer, batch)
    for copy in copies:
        copy.wait()
    for slot in range(slots):
        if slot > 0:

            @pl.when(slot < send_slots(meta_ref))
            def _():
                gather_rows(
                    index_ref, send_base(meta_ref, slot, slots, batch), batch, table, buffer, outs[slot - 1]
                )

        @pl.when(slot < own_slots(meta_ref))
        def _():
            gather_rows(
                index_ref, own_base(meta_ref, slot, slots, batch), batch, table, buffer, outs[slots - 1 + slot]
            )


def batch_kernel(
    batch, slots, slot, meta_ref, kinds_ref, relations_ref, remote_ref, local_ref, rel_in,
    remote_grad, local_grad, rel_out, source, target, queries, weights, diagonal, source_grad, target_grad,
):
    a, b, each = share(meta_ref)
    size, width = source.shape
    rel_count = relations_ref.shape[0]
    block = size // 2 if size % 512 == 0 else size
    inverse = 1.0 / (batch - 1)

    @pl.when(slot >= own_slots(meta_ref))
    def _():
        rel_out[...] = rel_in[...]

    @pl.when(slot < own_slots(meta_ref))
    def _():
        native = slot < b
        kinds = kinds_ref[pl.ds(jnp.where(native, slots + slot, each + slot - b), 1), :]
        source[...] = jnp.where(native, remote_ref[...], local_ref[...])
        target[...] = jnp.where(native, local_ref[...], remote_ref[...])
        full = relations_ref[...]
        high = full.astype(bf16)
        rest = full - high.astype(f32)
        middle = rest.astype(bf16)
        low = (rest - middle.astype(f32)).astype(bf16)
        kind_rows = lax.broadcasted_iota(jnp.int32, (rel_count, size), 0)
        onehot = jnp.where(kind_rows == kinds, 1.0, 0.0).astype(bf16)
        diagonal[...] = lax.dot_general(
            jnp.concatenate([onehot, onehot, onehot], axis=0),
            jnp.concatenate([high, middle, low], axis=0),
            (((0,), (0,)), ((), ())),
            preferred_element_type=f32,
        )
        queries[...] = (source[...].astype(f32) * diagonal[...]).astype(bf16)
        rel_grad = rel_in[...]
        on_diag = lax.broadcasted_iota(jnp.int32, (block, block), 0) == lax.broadcasted_iota(
            jnp.int32, (block, block), 1
        )
        for start in range(0, size, block):
            rows = pl.ds(start, block)
            scores = lax.dot_general(
                queries[rows, :], target[...], (((1,), (1,)), ((), ())), preferred_element_type=f32
            )
            probs = 0.5 * jnp.tanh(0.5 * scores) + 0.5
            weights[rows, :] = (probs * inverse).astype(bf16)
            square = probs[:, start : start + block]
            weights[rows, pl.ds(start, block)] = jnp.where(on_diag, square - 1.0, square * inverse).astype(bf16)
            grad_query = jnp.dot(weights[rows, :], target[...], preferred_element_type=f32)
            source_grad[rows, :] = grad_query * diagonal[rows, :]
            terms = grad_query * source[rows, :].astype(f32)
            terms_high = terms.astype(bf16)
            terms_low = (terms - terms_high.astype(f32)).astype(bf16)
            kind_part = onehot[:, start : start + block]
            rel_grad = (
                rel_grad
                + jnp.dot(kind_part, terms_high, preferred_element_type=f32)
                + jnp.dot(kind_part, terms_low, preferred_element_type=f32)
            )
        rel_out[...] = rel_grad
        for start in range(0, size, block):
            columns = pl.ds(start, block)
            target_grad[columns, :] = lax.dot_general(
                weights[:, columns], queries[...], (((0,), (0,)), ((), ())), preferred_element_type=f32
            )
        remote_grad[...] = jnp.where(native, source_grad[...], target_grad[...]).astype(bf16)
        for h in range(width // LANES):
            lanes = pl.ds(h * LANES, LANES)
            local_grad[h] = jnp.where(native, target_grad[:, lanes], source_grad[:, lanes])


def split_halves(grad_ref, buffer):
    for h in range(buffer.shape[0]):
        buffer[h] = grad_ref[:, h * LANES : (h + 1) * LANES].astype(f32)


def add_up(batch, slots, meta_ref, index_ref, *refs):
    local_grads, returned = refs[:slots], refs[slots : 2 * slots - 1]
    total, other_total, buffer = refs[2 * slots - 1 :]
    total[...] = jnp.zeros_like(total)
    other_total[...] = jnp.zeros_like(other_total)
    a, b, each = share(meta_ref)
    for slot in range(slots):

        @pl.when(slot < own_slots(meta_ref))
        def _():
            scatter_rows(
                index_ref, own_base(meta_ref, slot, slots, batch), batch, local_grads[slot], (total, other_total)
            )

        if slot < slots - 1:

            @pl.when((slot < send_slots(meta_ref)) & (slot < each - 1))
            def _():
                split_halves(returned[slot], buffer)
                scatter_rows(
                    index_ref, send_base(meta_ref, slot, slots, batch), batch, buffer, (total, other_total)
                )

    total[...] += other_total[...]


def update(
    batch, slots, more, meta_ref, index_ref, next_index_ref, grad_ref, rows_ref, state_ref, last_ref, *refs
):
    if more:
        new_rows, new_state, sent_ref, total, table, buffer, sems, out_sems = refs
    else:
        new_rows, new_state, total, table, buffer, sems, out_sems = refs
    halves, count, _ = total.shape
    width = halves * LANES
    grad_copy = pltpu.make_async_copy(grad_ref, total, sems.at[halves])
    grad_copy.start()
    copies = load_table(rows_ref, table, sems)
    for copy in copies:
        copy.start()
    clear_tail(buffer, batch)
    split_halves(last_ref, buffer)
    grad_copy.wait()
    a, b, each = share(meta_ref)

    @pl.when(each - 1 < send_slots(meta_ref))
    def _():
        scatter_rows(index_ref, send_base(meta_ref, each - 1, slots, batch), batch, buffer, (total,))

    for copy in copies:
        copy.wait()
    chunk = LANES
    group = 8 * chunk

    def out_copies(number):
        rows = pl.ds(number * group, group)
        return [
            pltpu.make_async_copy(
                table.at[h, rows, :], new_rows.at[rows, pl.ds(h * LANES, LANES)], out_sems.at[number, h]
            )
            for h in range(halves)
        ]

    for number in range(count // group):

        def step(i, carry):
            at = number * 8 + i
            rows = pl.ds(pl.multiple_of(at * chunk, chunk), chunk)
            grads = [total[h, rows, :] for h in range(halves)]
            squares = sum(g * g for g in grads)
            mean = jnp.sum(squares, axis=1, keepdims=True) * (1.0 / width)
            old = jnp.broadcast_to(state_ref[pl.ds(at, 1), :], (chunk, LANES))
            now = jnp.transpose(old) + mean
            factor = learn_rate * lax.rsqrt(now)
            for h in range(halves):
                table[h, rows, :] = table[h, rows, :] - grads[h] * factor
            new_state[pl.ds(at, 1), :] = jnp.transpose(now)[0:1, :]
            return carry

        lax.fori_loop(0, 8, step, 0)
        for copy in out_copies(number):
            copy.start()
    if more:
        clear_tail(buffer, batch)
        gather_rows(next_index_ref, 0, batch, table, buffer, sent_ref)
    for number in range(count // group):
        for copy in out_copies(number):
            copy.wait()


def params(mib):
    return pltpu.CompilerParams(vmem_limit_bytes=mib * MIB)


def on_device(
    embeddings, row_state, relations, rel_state, edge_src, edge_dst, edge_rel, batch_count
):
    bit_count = lax.axis_size("dom").bit_length() - 1
    row_count, width = embeddings.shape
    rounds, slots, batch = edge_src.shape[2:]
    rel_count = relations.shape[0]
    halves = width // LANES
    size = -(-batch // 256) * 256
    rows_shape = jax.ShapeDtypeStruct((size, width), bf16)
    table_scratch = pltpu.VMEM((halves, row_count, LANES), f32)
    slot_scratch = pltpu.VMEM((halves, size, LANES), f32)
    swaps = [1 << (bit_count - 1 - number) for number in range(ROUNDS)]
    lists = []
    for number in range(ROUNDS):
        sources = edge_src[0, 0, number].reshape(-1)
        mine = jnp.concatenate(
            [edge_dst[0, 0, number].reshape(-1), edge_rel[0, 0, number].reshape(-1), batch_count[0, 0, number][None]]
        )
        theirs = from_partner(mine, "dom", swaps[number])
        targets = theirs[: slots * batch]
        their_kinds = theirs[slots * batch : 2 * slots * batch].reshape(slots, batch)
        kinds = jnp.concatenate([edge_rel[0, 0, number], their_kinds], axis=0)
        kinds = jnp.pad(kinds, ((0, 0), (0, size - batch)), constant_values=-1)
        meta = jnp.stack([batch_count[0, 0, number], theirs[2 * slots * batch]])
        lists.append((sources, jnp.concatenate([sources, targets]), kinds, meta))

    state = row_state.reshape(row_count // LANES, LANES)
    sent = pl.pallas_call(
        functools.partial(first_gather, batch),
        out_shape=rows_shape,
        in_specs=[SMEM_SPEC, ANY_SPEC],
        out_specs=VMEM_SPEC,
        scratch_shapes=[table_scratch, slot_scratch, pltpu.SemaphoreType.DMA((halves,))],
        compiler_params=params(20),
        name="first_gather",
    )(lists[0][0], embeddings)

    for number in range(ROUNDS):
        swap = swaps[number]
        _, index, kinds, meta = lists[number]
        got_first = from_partner(sent, "dom", swap)
        gathered = pl.pallas_call(
            functools.partial(other_gathers, batch, slots),
            out_shape=[rows_shape] * (2 * slots - 1),
            in_specs=[SMEM_SPEC, SMEM_SPEC, ANY_SPEC],
            out_specs=[VMEM_SPEC] * (2 * slots - 1),
            scratch_shapes=[table_scratch, slot_scratch, pltpu.SemaphoreType.DMA((halves,))],
            compiler_params=params(30),
            name="other_gathers",
        )(meta, index, embeddings)
        to_send, local_rows = gathered[: slots - 1], gathered[slots - 1 :]

        def run_batch(slot, meta, kinds, relations, remote, local, rel_grad):
            return pl.pallas_call(
                functools.partial(batch_kernel, batch, slots, slot),
                out_shape=[
                    rows_shape,
                    jax.ShapeDtypeStruct((halves, size, LANES), f32),
                    jax.ShapeDtypeStruct(relations.shape, f32),
                ],
                in_specs=[SMEM_SPEC] + [VMEM_SPEC] * 5,
                out_specs=[VMEM_SPEC] * 3,
                scratch_shapes=[
                    pltpu.VMEM((size, width), bf16),
                    pltpu.VMEM((size, width), bf16),
                    pltpu.VMEM((size, width), bf16),
                    pltpu.VMEM((size, size), bf16),
                    pltpu.VMEM((size, width), f32),
                    pltpu.VMEM((size, width), f32),
                    pltpu.VMEM((size, width), f32),
                ],
                compiler_params=params(24),
                cost_estimate=pl.CostEstimate(
                    flops=6 * size * size * width, bytes_accessed=8 * size * width, transcendentals=size * size
                ),
                name="batch",
            )(meta, kinds, relations, remote, local, rel_grad)

        def branch(used):
            def run(got_first, to_send, local_rows, meta, kinds, relations):
                got = [got_first] + [from_partner(to_send[n], "dom", swap) for n in range(used - 1)]
                rel_grad = jnp.zeros(relations.shape, f32)
                local_grads, returned, last = [], [], None
                for slot in range(used):
                    last, local_grad, rel_grad = run_batch(
                        slot, meta, kinds, relations, got[slot], local_rows[slot], rel_grad
                    )
                    local_grads.append(local_grad)
                    if slot < used - 1:
                        returned.append(from_partner(last, "dom", swap))
                for _ in range(used, slots):
                    local_grads.append(jnp.zeros((halves, size, LANES), f32))
                    returned.append(jnp.zeros((size, width), bf16))
                return tuple(local_grads), tuple(returned), last, rel_grad

            return run

        each = (meta[0] + meta[1] + 1) // 2
        local_grads, returned, last, rel_grad = lax.switch(
            each - 1,
            [branch(used) for used in range(1, slots + 1)],
            got_first, to_send, local_rows, meta, kinds, relations,
        )
        got_last = from_partner(last, "dom", swap)
        grads = pl.pallas_call(
            functools.partial(add_up, batch, slots),
            out_shape=jax.ShapeDtypeStruct((halves, row_count, LANES), f32),
            in_specs=[SMEM_SPEC] * 2 + [VMEM_SPEC] * (2 * slots - 1),
            out_specs=VMEM_SPEC,
            scratch_shapes=[table_scratch, slot_scratch],
            compiler_params=params(40),
            name="add_up",
        )(meta, index, *local_grads, *returned)
        rel_total = sum_over(sum_over(rel_grad, "rep"), "dom")
        more = number + 1 < ROUNDS
        outs = pl.pallas_call(
            functools.partial(update, batch, slots, more),
            out_shape=[
                jax.ShapeDtypeStruct(embeddings.shape, f32),
                jax.ShapeDtypeStruct(state.shape, f32),
            ]
            + [rows_shape] * more,
            in_specs=[SMEM_SPEC] * 3 + [ANY_SPEC, ANY_SPEC, VMEM_SPEC, VMEM_SPEC],
            out_specs=[ANY_SPEC, VMEM_SPEC] + [VMEM_SPEC] * more,
            scratch_shapes=[
                table_scratch,
                table_scratch,
                slot_scratch,
                pltpu.SemaphoreType.DMA((halves + 1,)),
                pltpu.SemaphoreType.DMA((row_count // (8 * LANES), halves)),
            ],
            compiler_params=params(30),
            name="update",
        )(meta, index, lists[(number + 1) % ROUNDS][0], grads, embeddings, state, got_last)
        if more:
            embeddings, state, sent = outs
        else:
            embeddings, state = outs
        rel_state = rel_state + rel_total * rel_total
        relations = relations - rel_rate * rel_total / jnp.sqrt(rel_state)
    return (embeddings, state.reshape(row_count), relations, rel_state)


def solution(mesh):
    return jax.shard_map(
        on_device,
        mesh=mesh,
        in_specs=(
            P(("dom", "rep"), None),
            P(("dom", "rep")),
            P(),
            P(),
            P("dom", "rep", None, None, None),
            P("dom", "rep", None, None, None),
            P("dom", "rep", None, None, None),
            P("dom", "rep", None),
        ),
        out_specs=(P(("dom", "rep"), None), P(("dom", "rep")), P(), P()),
        check_vma=False,
    )
```

```python
import functools

import jax
import jax.numpy as jnp
from jax import lax
from jax.experimental import pallas as pl
from jax.experimental.pallas import tpu as pltpu
from jax.sharding import PartitionSpec as P

ROUNDS = 2


learn_rate = 0.1
rel_rate = 0.1

f32 = jnp.float32
bf16 = jnp.bfloat16
MIB = 1 << 20
LANES = 128
SMEM_SPEC = pl.BlockSpec(memory_space=pltpu.SMEM)
VMEM_SPEC = pl.BlockSpec(memory_space=pltpu.VMEM)
ANY_SPEC = pl.BlockSpec(memory_space=pl.ANY)
HBM_SPEC = pl.BlockSpec(memory_space=pltpu.HBM)


def from_partner(shard, axis, distance, senders=(0, 1)):
    pairs = [(i, i ^ distance) for i in range(lax.axis_size(axis)) if (i & distance != 0) in senders]
    return lax.ppermute(shard, axis, pairs)


def sum_over(values, axis):
    for bit in range(lax.axis_size(axis).bit_length() - 1):
        values = values + from_partner(values, axis, 1 << bit)
    return values


def unroll_of(count):
    return max(d for d in range(1, 41) if count % d == 0)


def share(meta_ref):
    a, b = meta_ref[0], meta_ref[1]
    return a, b, (a + b + 1) // 2


def send_slots(meta_ref):
    a, b, each = share(meta_ref)
    return jnp.minimum(a, each) + jnp.maximum(b - each, 0)


def own_slots(meta_ref):
    a, b, each = share(meta_ref)
    return jnp.minimum(b, each) + jnp.maximum(a - each, 0)


def send_base(meta_ref, slot, slots, batch):
    a, b, each = share(meta_ref)
    return jnp.where(slot < a, slot, slots + each + slot - a) * batch


def own_base(meta_ref, slot, slots, batch):
    a, b, each = share(meta_ref)
    return jnp.where(slot < b, slots + slot, each + slot - b) * batch


def gather_rows(index_ref, base, batch, table, buffer, out_ref):
    unroll = unroll_of(batch)
    halves, size, _ = buffer.shape
    if size > batch:
        buffer[:, batch:, :] = jnp.zeros((halves, size - batch, LANES), f32)

    def step(i, carry):
        at = i * unroll
        for u in range(unroll):
            row = index_ref[base + at + u]
            for h in range(halves):
                buffer[h, pl.ds(at + u, 1), :] = table[h, pl.ds(row, 1), :]
        return carry

    lax.fori_loop(0, batch // unroll, step, 0)
    for h in range(halves):
        out_ref[:, h * LANES : (h + 1) * LANES] = buffer[h].astype(bf16)


def scatter_rows(index_ref, base, batch, grads, totals):
    unroll = unroll_of(batch)

    def step(i, carry):
        at = i * unroll
        for u in range(unroll):
            row = index_ref[base + at + u]
            for h, total in enumerate(totals):
                total[pl.ds(row, 1), :] += grads[h, pl.ds(at + u, 1), :]
        return carry

    lax.fori_loop(0, batch // unroll, step, 0)


def load_table(rows_ref, table, sems):
    return [
        pltpu.make_async_copy(rows_ref.at[:, pl.ds(h * LANES, LANES)], table.at[h], sems.at[h])
        for h in range(table.shape[0])
    ]


def load_kernel(batch, index_ref, rows_ref, table, sent_ref, buffer, sems):
    copies = load_table(rows_ref, table, sems)
    for copy in copies:
        copy.start()
    for copy in copies:
        copy.wait()
    gather_rows(index_ref, 0, batch, table, buffer, sent_ref)


def first_kernel(batch, index_ref, table, sent_ref, buffer):
    gather_rows(index_ref, 0, batch, table, buffer, sent_ref)


def send_kernel(batch, slots, meta_ref, index_ref, table, *refs):
    outs, buffer = refs[:-1], refs[-1]
    for slot in range(1, slots):

        @pl.when(slot < send_slots(meta_ref))
        def _():
            gather_rows(index_ref, send_base(meta_ref, slot, slots, batch), batch, table, buffer, outs[slot - 1])


def own_kernel(batch, slots, meta_ref, index_ref, table, *refs):
    outs, buffer = refs[:-1], refs[-1]
    for slot in range(slots):

        @pl.when(slot < own_slots(meta_ref))
        def _():
            gather_rows(index_ref, own_base(meta_ref, slot, slots, batch), batch, table, buffer, outs[slot])


def batch_kernel(
    batch, slots, slot, meta_ref, kinds_ref, relations_ref, remote_ref, local_ref, rel_in,
    remote_grad, local_grad, rel_out, source, target, queries, weights, diagonal, source_grad, target_grad,
):
    a, b, each = share(meta_ref)
    size, width = source.shape
    sent = remote_ref.shape[0]
    rel_count = relations_ref.shape[0]
    block = size // 2 if size % 512 == 0 else size
    inverse = 1.0 / (batch - 1)

    @pl.when(slot >= own_slots(meta_ref))
    def _():
        rel_out[...] = rel_in[...]

    @pl.when(slot < own_slots(meta_ref))
    def _():
        native = slot < b
        kinds = kinds_ref[pl.ds(jnp.where(native, slots + slot, each + slot - b), 1), :]
        source[:sent, :] = jnp.where(native, remote_ref[...], local_ref[...])
        target[:sent, :] = jnp.where(native, local_ref[...], remote_ref[...])
        if size > sent:
            source[sent:, :] = jnp.zeros((size - sent, width), bf16)
            target[sent:, :] = jnp.zeros((size - sent, width), bf16)
        full = relations_ref[...]
        high = full.astype(bf16)
        rest = full - high.astype(f32)
        middle = rest.astype(bf16)
        low = (rest - middle.astype(f32)).astype(bf16)
        kind_rows = lax.broadcasted_iota(jnp.int32, (rel_count, size), 0)
        onehot = jnp.where(kind_rows == kinds, 1.0, 0.0).astype(bf16)
        diagonal[...] = lax.dot_general(
            jnp.concatenate([onehot, onehot, onehot], axis=0),
            jnp.concatenate([high, middle, low], axis=0),
            (((0,), (0,)), ((), ())),
            preferred_element_type=f32,
        )
        queries[...] = (source[...].astype(f32) * diagonal[...]).astype(bf16)
        rel_grad = rel_in[...]
        on_diag = lax.broadcasted_iota(jnp.int32, (block, block), 0) == lax.broadcasted_iota(
            jnp.int32, (block, block), 1
        )
        for start in range(0, size, block):
            rows = pl.ds(start, block)
            scores = lax.dot_general(
                queries[rows, :], target[...], (((1,), (1,)), ((), ())), preferred_element_type=f32
            )
            probs = 0.5 * jnp.tanh(0.5 * scores) + 0.5
            weights[rows, :] = (probs * inverse).astype(bf16)
            square = probs[:, start : start + block]
            weights[rows, pl.ds(start, block)] = jnp.where(on_diag, square - 1.0, square * inverse).astype(bf16)
            grad_query = jnp.dot(weights[rows, :], target[...], preferred_element_type=f32)
            source_grad[rows, :] = grad_query * diagonal[rows, :]
            terms = grad_query * source[rows, :].astype(f32)
            terms_high = terms.astype(bf16)
            terms_low = (terms - terms_high.astype(f32)).astype(bf16)
            kind_part = onehot[:, start : start + block]
            rel_grad = (
                rel_grad
                + jnp.dot(kind_part, terms_high, preferred_element_type=f32)
                + jnp.dot(kind_part, terms_low, preferred_element_type=f32)
            )
        rel_out[...] = rel_grad
        for start in range(0, size, block):
            columns = pl.ds(start, block)
            target_grad[columns, :] = lax.dot_general(
                weights[:, columns], queries[...], (((0,), (0,)), ((), ())), preferred_element_type=f32
            )
        remote_grad[...] = jnp.where(native, source_grad[:sent, :], target_grad[:sent, :]).astype(bf16)
        for h in range(width // LANES):
            lanes = pl.ds(h * LANES, LANES)
            local_grad[h] = jnp.where(native, target_grad[:sent, lanes], source_grad[:sent, lanes])


def clear_kernel(*totals):
    for total in totals:
        total[...] = jnp.zeros_like(total)


def add_returned(batch, slots, slot, meta_ref, index_ref, returned_ref, totals, buffer):
    for h in range(buffer.shape[0]):
        buffer[h] = returned_ref[:, h * LANES : (h + 1) * LANES].astype(f32)
    scatter_rows(index_ref, send_base(meta_ref, slot, slots, batch), batch, buffer, totals)


def add_kernel(batch, slots, slot, halves, meta_ref, index_ref, grads, returned_ref, *refs):
    totals, buffer = refs[halves : 2 * halves], refs[2 * halves]

    @pl.when(slot < own_slots(meta_ref))
    def _():
        scatter_rows(index_ref, own_base(meta_ref, slot, slots, batch), batch, grads, totals)

    @pl.when(slot < send_slots(meta_ref) - 1)
    def _():
        add_returned(batch, slots, slot, meta_ref, index_ref, returned_ref, totals, buffer)


def update_kernel(batch, slots, halves, meta_ref, index_ref, last_ref, state_ref, rows_ref, *refs):
    totals, refs = refs[halves : 2 * halves], refs[2 * halves :]
    table, new_state, new_rows, buffer, sems, out_sems = refs
    copies = load_table(rows_ref, table, sems)
    for copy in copies:
        copy.start()
    count = table.shape[1]
    width = halves * LANES
    add_returned(batch, slots, send_slots(meta_ref) - 1, meta_ref, index_ref, last_ref, totals, buffer)
    for copy in copies:
        copy.wait()
    chunk = LANES
    unroll = 8
    group = unroll * chunk

    def out_copies(number):
        rows = pl.ds(number * group, group)
        return [
            pltpu.make_async_copy(
                table.at[h, rows, :], new_rows.at[rows, pl.ds(h * LANES, LANES)], out_sems.at[number, h]
            )
            for h in range(halves)
        ]

    def update_group(number):
        for u in range(unroll):
            at = number * unroll + u
            rows = pl.ds(at * chunk, chunk)
            grads = [total[rows, :] for total in totals]
            squares = sum(g * g for g in grads)
            mean = jnp.sum(jnp.transpose(squares), axis=0, keepdims=True) * (1.0 / width)
            now = state_ref[pl.ds(at, 1), :] + mean
            new_state[pl.ds(at, 1), :] = now
            factor = jnp.transpose(jnp.broadcast_to(learn_rate * lax.rsqrt(now), (chunk, LANES)))
            for h in range(halves):
                table[h, rows, :] = table[h, rows, :] - grads[h] * factor

    for number in range(count // group):
        update_group(number)
        for copy in out_copies(number):
            copy.start()
    for number in range(count // group):
        for copy in out_copies(number):
            copy.wait()


def params(mib):
    return pltpu.CompilerParams(vmem_limit_bytes=mib * MIB)


def in_vmem(array):
    return pltpu.with_memory_space_constraint(array, pltpu.VMEM)


def in_hbm(array):
    return pltpu.with_memory_space_constraint(array, pltpu.HBM)


def cost(us):
    return pl.CostEstimate(flops=0, bytes_accessed=int(us * 3.4e6), transcendentals=0)


def on_device(
    embeddings, row_state, relations, rel_state, edge_src, edge_dst, edge_rel, batch_count
):
    bit_count = lax.axis_size("dom").bit_length() - 1
    row_count, width = embeddings.shape
    slots, batch = edge_src.shape[3:]
    halves = width // LANES
    size = -(-batch // 256) * 256
    sent_size = -(-batch // 16) * 16
    sent_shape = jax.ShapeDtypeStruct((sent_size, width), bf16)
    half_shape = jax.ShapeDtypeStruct((halves, sent_size, LANES), f32)
    table_shape = pltpu.VMEM((halves, row_count, LANES), f32)
    plane_shape = pltpu.VMEM((row_count, LANES), f32)
    buffer = pltpu.VMEM(half_shape.shape, f32)
    swaps = [1 << (bit_count - 1 - number) for number in range(ROUNDS)]

    state = row_state.reshape(row_count // LANES, LANES)
    sources = [edge_src[0, 0, number].reshape(-1) for number in range(ROUNDS)]
    table, sent = pl.pallas_call(
        functools.partial(load_kernel, batch),
        out_shape=[table_shape, sent_shape],
        in_specs=[SMEM_SPEC, HBM_SPEC],
        out_specs=[VMEM_SPEC] * 2,
        scratch_shapes=[buffer, pltpu.SemaphoreType.DMA((halves,))],
        compiler_params=params(16),
        cost_estimate=cost(5),
        name="load_and_gather",
    )(sources[0], in_hbm(embeddings))
    sent, edge_dst, edge_rel, batch_count = lax.optimization_barrier((sent, edge_dst, edge_rel, batch_count))
    got_first = from_partner(sent, "dom", swaps[0])

    lists = []
    for number in range(ROUNDS):
        mine = jnp.concatenate(
            [edge_dst[0, 0, number].reshape(-1), edge_rel[0, 0, number].reshape(-1), batch_count[0, 0, number][None]]
        )
        theirs = from_partner(mine, "dom", swaps[number])
        targets = theirs[: slots * batch]
        their_kinds = theirs[slots * batch : 2 * slots * batch].reshape(slots, batch)
        kinds = jnp.concatenate([edge_rel[0, 0, number], their_kinds], axis=0)
        kinds = jnp.pad(kinds, ((0, 0), (0, size - batch)), constant_values=-1)
        meta = jnp.stack([batch_count[0, 0, number], theirs[2 * slots * batch]])
        lists.append((jnp.concatenate([sources[number], targets]), kinds, meta))
    lists = lax.optimization_barrier(lists)

    for number in range(ROUNDS):
        swap = swaps[number]
        index, kinds, meta = lists[number]
        if number > 0:
            sent = pl.pallas_call(
                functools.partial(first_kernel, batch),
                out_shape=sent_shape,
                in_specs=[SMEM_SPEC, VMEM_SPEC],
                out_specs=VMEM_SPEC,
                scratch_shapes=[buffer],
                compiler_params=params(16),
                cost_estimate=cost(2),
                name="first_gather",
            )(index, in_vmem(table))
            got_first = from_partner(sent, "dom", swap)
        to_send = pl.pallas_call(
            functools.partial(send_kernel, batch, slots),
            out_shape=[sent_shape] * (slots - 1),
            in_specs=[SMEM_SPEC, SMEM_SPEC, VMEM_SPEC],
            out_specs=[VMEM_SPEC] * (slots - 1),
            scratch_shapes=[buffer],
            compiler_params=params(16),
            cost_estimate=cost(4),
            name="send_gathers",
        )(meta, index, in_vmem(table))
        local_rows = pl.pallas_call(
            functools.partial(own_kernel, batch, slots),
            out_shape=[sent_shape] * slots,
            in_specs=[SMEM_SPEC, SMEM_SPEC, VMEM_SPEC],
            out_specs=[VMEM_SPEC] * slots,
            scratch_shapes=[buffer],
            compiler_params=params(16),
            cost_estimate=cost(5),
            name="own_gathers",
        )(meta, index, in_vmem(table))

        def run_batch(slot, meta, kinds, relations, remote, local, rel_grad):
            return pl.pallas_call(
                functools.partial(batch_kernel, batch, slots, slot),
                out_shape=[sent_shape, half_shape, jax.ShapeDtypeStruct(relations.shape, f32)],
                in_specs=[SMEM_SPEC] + [VMEM_SPEC] * 5,
                out_specs=[VMEM_SPEC] * 3,
                scratch_shapes=[pltpu.VMEM((size, width), bf16)] * 3
                + [pltpu.VMEM((size, size), bf16)]
                + [pltpu.VMEM((size, width), f32)] * 3,
                compiler_params=params(16),
                cost_estimate=cost(4),
                name="batch",
            )(meta, kinds, relations, remote, local, rel_grad)

        def branch(low_sends, high_sends):
            most, least = max(low_sends, high_sends), min(low_sends, high_sends)
            one_way = (0,) if low_sends > high_sends else (1,)
            way_back = (1,) if low_sends > high_sends else (0,)

            def run(got_first, to_send, local_rows, meta, kinds, relations):
                got = [got_first] + [
                    from_partner(to_send[n], "dom", swap, (0, 1) if n + 1 < least else one_way)
                    for n in range(most - 1)
                ]
                rel_grad = jnp.zeros(relations.shape, f32)
                returned, remote_grads, local_grads = [], [], []
                for slot in range(most):
                    remote_grad, local_grad, rel_grad = run_batch(
                        slot, meta, kinds, relations, got[slot], local_rows[slot], rel_grad
                    )
                    remote_grads.append(remote_grad)
                    local_grads.append(local_grad)
                    if slot < most - 1:
                        back = (0, 1) if slot < least - 1 else way_back
                        returned.append(from_partner(remote_grad, "dom", swap, back))
                local_grads += [jnp.zeros(half_shape.shape, f32)] * (slots - most)
                returned += [jnp.zeros(sent_shape.shape, bf16)] * (slots - most)
                last = remote_grads[-1]
                if most > least:
                    bit = lax.axis_index("dom") & swap != 0
                    last = jnp.where(bit == (way_back[0] == 1), last, remote_grads[-2])
                return last, rel_grad, local_grads, returned

            return run

        pairs = []
        for total in range(2, 2 * slots + 1):
            pairs += [(total // 2, total - total // 2)]
            pairs += [(total - total // 2, total // 2)] * (total % 2)
        sends = jnp.minimum(meta[0], (meta[0] + meta[1] + 1) // 2)
        sends = sends + jnp.maximum(meta[1] - (meta[0] + meta[1] + 1) // 2, 0)
        both = meta[0] + meta[1]
        high_side = lax.axis_index("dom") & swap != 0
        low_sends = jnp.where(high_side, both - sends, sends)
        place = sum(
            jnp.where((both == low + high) & (low_sends == low), n, 0) for n, (low, high) in enumerate(pairs)
        )
        last, rel_grad, local_grads, returned = lax.switch(
            place,
            [branch(low, high) for low, high in pairs],
            got_first, to_send, local_rows, meta, kinds, relations,
        )
        got_last = from_partner(last, "dom", swap)
        rel_total = sum_over(sum_over(rel_grad, "rep"), "dom")
        totals = pl.pallas_call(
            clear_kernel,
            out_shape=[plane_shape] * halves,
            out_specs=[VMEM_SPEC] * halves,
            compiler_params=params(16),
            cost_estimate=cost(1),
            name="clear",
        )()
        for slot in range(slots):
            totals = pl.pallas_call(
                functools.partial(add_kernel, batch, slots, slot, halves),
                out_shape=[plane_shape] * halves,
                in_specs=[SMEM_SPEC] * 2 + [VMEM_SPEC] * (2 + halves),
                out_specs=[VMEM_SPEC] * halves,
                scratch_shapes=[buffer],
                input_output_aliases={4 + h: h for h in range(halves)},
                compiler_params=params(16),
                cost_estimate=cost(4),
                name="add_rows",
            )(meta, index, local_grads[slot], returned[min(slot, slots - 2)], *map(in_vmem, totals))
        outs = pl.pallas_call(
            functools.partial(update_kernel, batch, slots, halves),
            out_shape=[plane_shape] * halves
            + [table_shape, jax.ShapeDtypeStruct(state.shape, f32), jax.ShapeDtypeStruct(embeddings.shape, f32)],
            in_specs=[SMEM_SPEC] * 2 + [VMEM_SPEC] * 2 + [HBM_SPEC] + [VMEM_SPEC] * halves,
            out_specs=[VMEM_SPEC] * (2 + halves) + [HBM_SPEC],
            scratch_shapes=[
                buffer,
                pltpu.SemaphoreType.DMA((halves,)),
                pltpu.SemaphoreType.DMA((row_count // (8 * LANES), halves)),
            ],
            input_output_aliases={5 + h: h for h in range(halves)},
            compiler_params=params(16),
            cost_estimate=cost(8),
            name="update",
        )(meta, index, got_last, state, in_hbm(embeddings), *map(in_vmem, totals))
        table, state, embeddings = outs[halves:]
        rel_state = rel_state + rel_total * rel_total
        relations = relations - rel_rate * rel_total / jnp.sqrt(rel_state)
    return (embeddings, state.reshape(row_count), relations, rel_state)


def solution(mesh):
    return jax.shard_map(
        on_device,
        mesh=mesh,
        in_specs=(
            P(("dom", "rep"), None),
            P(("dom", "rep")),
            P(),
            P(),
            P("dom", "rep", None, None, None),
            P("dom", "rep", None, None, None),
            P("dom", "rep", None, None, None),
            P("dom", "rep", None),
        ),
        out_specs=(P(("dom", "rep"), None), P(("dom", "rep")), P(), P()),
        check_vma=False,
    )
```

```python
import functools

import jax
import jax.numpy as jnp
from jax import lax
from jax.experimental import pallas as pl
from jax.experimental.pallas import tpu as pltpu
from jax.sharding import PartitionSpec as P

ROUNDS = 2


learn_rate = 0.1
rel_rate = 0.1

f32 = jnp.float32
bf16 = jnp.bfloat16
MIB = 1 << 20
LANES = 128
SUMS = 3
SMEM_SPEC = pl.BlockSpec(memory_space=pltpu.SMEM)
VMEM_SPEC = pl.BlockSpec(memory_space=pltpu.VMEM)
ANY_SPEC = pl.BlockSpec(memory_space=pl.ANY)
HBM_SPEC = pl.BlockSpec(memory_space=pltpu.HBM)


def from_partner(shard, axis, distance, senders=(0, 1)):
    pairs = [(i, i ^ distance) for i in range(lax.axis_size(axis)) if (i & distance != 0) in senders]
    return lax.ppermute(shard, axis, pairs)


def unroll_of(count):
    return max(d for d in range(1, 41) if count % d == 0)


def task_list(meta_ref, task, slots):
    own, theirs, low = meta_ref[0], meta_ref[1], meta_ref[2] == 1
    if isinstance(task, int) and task < 2:
        return task == 0, task * slots
    first = jnp.where(low, own, theirs) - 1
    is_first = task - 2 < first
    number = jnp.where(is_first, task - 1, task - 1 - first)
    is_own = is_first == low
    return is_own, jnp.where(is_own, number, slots + number)


def task_count(meta_ref):
    return meta_ref[0] + meta_ref[1]


def fetch_list(lists_ref, number, list_ref, sem):
    size = list_ref.shape[0]
    return pltpu.make_async_copy(lists_ref.at[pl.ds(pl.multiple_of(number * size, size), size)], list_ref, sem)


def gather_rows(batch, list_ref, table, buffer, out_ref):
    unroll = unroll_of(batch)
    halves, size, _ = buffer.shape
    if size > batch:
        buffer[:, batch:, :] = jnp.zeros((halves, size - batch, LANES), f32)

    def step(i, carry):
        at = i * unroll
        for u in range(unroll):
            row = list_ref[at + u]
            for h in range(halves):
                buffer[h, pl.ds(at + u, 1), :] = table[h, pl.ds(row, 1), :]
        return carry

    lax.fori_loop(0, batch // unroll, step, 0)
    for h in range(halves):
        out_ref[:size, h * LANES : (h + 1) * LANES] = buffer[h].astype(bf16)


def scatter_rows(batch, halves, list_ref, grads, totals):
    unroll = unroll_of(batch)

    def step(i, carry):
        at = i * unroll
        for u in range(unroll):
            row = pl.ds(pl.multiple_of(list_ref[at + u] * halves, halves), halves)
            totals[u % SUMS][row, :] += grads[pl.ds(pl.multiple_of((at + u) * halves, halves), halves), :]
        return carry

    lax.fori_loop(0, batch // unroll, step, 0)


def load_table(rows_ref, table, sems):
    return [
        pltpu.make_async_copy(rows_ref.at[:, pl.ds(h * LANES, LANES)], table.at[h], sems.at[h])
        for h in range(table.shape[0])
    ]


def load_kernel(batch, lists_ref, rows_ref, table, sent_ref, buffer, list_ref, list_sem, sems):
    copies = load_table(rows_ref, table, sems) + [fetch_list(lists_ref, 0, list_ref, list_sem)]
    for copy in copies:
        copy.start()
    for copy in copies:
        copy.wait()
    gather_rows(batch, list_ref, table, buffer, sent_ref)


def gather_kernel(batch, slots, tasks, meta_ref, lists_ref, table, *refs):
    outs, (buffer, *held, sems) = refs[: len(tasks)], refs[len(tasks) :]
    copies = [
        fetch_list(lists_ref, task_list(meta_ref, task, slots)[1], held[n], sems.at[n])
        for n, task in enumerate(tasks)
    ]
    for n, task in enumerate(tasks):
        pl.when(task < task_count(meta_ref))(copies[n].start)
    for n, task in enumerate(tasks):

        @pl.when(task < task_count(meta_ref))
        def _():
            copies[n].wait()
            gather_rows(batch, held[n], table, buffer, outs[n])


def batch_task(
    batch, live, is_own, number, kinds_ref, relations_ref, local, remote, rel_out, out_ref, left, right, weights, scale
):
    size, width = left.shape
    halves = width // LANES
    sent = local.shape[0]
    rel_count = relations_ref.shape[0]
    block = size
    inverse = 1.0 / (batch - 1)

    @pl.when(live)
    def _():
        kinds = kinds_ref[pl.ds(number, 1), :]
        full = relations_ref[...]
        high = full.astype(bf16)
        rest = full - high.astype(f32)
        middle = rest.astype(bf16)
        low = (rest - middle.astype(f32)).astype(bf16)
        kind_rows = lax.broadcasted_iota(jnp.int32, (rel_count, size), 0)
        onehot = jnp.where(kind_rows == kinds, 1.0, 0.0).astype(bf16)
        diagonal = lax.dot_general(
            jnp.concatenate([onehot, onehot, onehot], axis=0),
            jnp.concatenate([high, middle, low], axis=0),
            (((0,), (0,)), ((), ())),
            preferred_element_type=f32,
        )
        scale[...] = jnp.where(is_own, diagonal, 1.0)
        left[:sent, :] = (local[...].astype(f32) * scale[:sent, :]).astype(bf16)
        right[:sent, :] = (remote[...].astype(f32) * jnp.where(is_own, 1.0, diagonal[:sent, :])).astype(bf16)
        if size > sent:
            left[sent:, :] = jnp.zeros((size - sent, width), bf16)
            right[sent:, :] = jnp.zeros((size - sent, width), bf16)
        rel_grad = rel_out[...]
        on_diag = lax.broadcasted_iota(jnp.int32, (block, block), 0) == lax.broadcasted_iota(
            jnp.int32, (block, block), 1
        )
        for start in range(0, size, block):
            rows = pl.ds(start, block)
            scores = lax.dot_general(
                left[rows, :], right[...], (((1,), (1,)), ((), ())), preferred_element_type=f32
            )
            probs = 0.5 * jnp.tanh(0.5 * scores) + 0.5
            weights[...] = (probs * inverse).astype(bf16)
            square = probs[:, start : start + block]
            weights[:, pl.ds(start, block)] = jnp.where(on_diag, square - 1.0, square * inverse).astype(bf16)
            grads = jnp.dot(weights[...], right[...], preferred_element_type=f32)
            stop = min(start + block, sent)
            used = stop - start
            scaled = grads * scale[rows, :]
            for h in range(halves):
                out_ref[pl.ds(start * halves + h, used, stride=halves), :] = scaled[
                    :used, h * LANES : (h + 1) * LANES
                ]
            own_rows = local[start:stop, :].astype(f32)
            terms = jnp.where(is_own, grads[:used, :] * own_rows, 0.0)
            terms_high = terms.astype(bf16)
            terms_low = (terms - terms_high.astype(f32)).astype(bf16)
            kind_part = onehot[:, start:stop]
            rel_grad = (
                rel_grad
                + jnp.dot(kind_part, terms_high, preferred_element_type=f32)
                + jnp.dot(kind_part, terms_low, preferred_element_type=f32)
            )
        rel_out[...] = rel_grad


def pair_kernel(
    batch, slots, tasks, meta_ref, kinds_ref, relations_ref, local_a, local_b, remote_a, remote_b, rel_in,
    rel_out, out_a, out_b, left, right, weights, scale,
):
    rel_out[...] = rel_in[...]
    for task, mine, theirs, out_ref in ((tasks[0], local_a, remote_a, out_a), (tasks[1], local_b, remote_b, out_b)):
        is_own, number = task_list(meta_ref, task, slots)
        batch_task(
            batch, task < task_count(meta_ref), is_own, number, kinds_ref, relations_ref, mine, theirs, rel_out,
            out_ref, left, right, weights, scale,
        )


def last_kernel(batch, slots, pairs, meta_ref, kinds_ref, relations_ref, rel_in, *refs):
    mine, theirs, refs = refs[: 2 * pairs], refs[2 * pairs : 4 * pairs], refs[4 * pairs :]
    rel_out, out_a, out_b, left, right, weights, scale, local, remote, sems = refs
    rel_out[...] = rel_in[...]
    last = (task_count(meta_ref) - 1) >> 1
    tasks = [2 * last, 2 * last + 1]

    def copies(part, pair):
        return [
            pltpu.make_async_copy(mine[2 * pair + part], local.at[part], sems.at[part, 0]),
            pltpu.make_async_copy(theirs[2 * pair + part], remote.at[part], sems.at[part, 1]),
        ]

    for part, task in enumerate(tasks):
        for pair in range(pairs):

            @pl.when((task < task_count(meta_ref)) & (last == pair))
            def _():
                for copy in copies(part, pair):
                    copy.start()

    for part, (task, out_ref) in enumerate(zip(tasks, (out_a, out_b))):
        live = task < task_count(meta_ref)

        @pl.when(live)
        def _():
            for copy in copies(part, 0):
                copy.wait()

        is_own, number = task_list(meta_ref, task, slots)
        is_own = jnp.where(task < 2, task, jnp.where(is_own, 0, 1)) == 0
        number = jnp.where(task < 2, task * slots, number)
        batch_task(
            batch, live, is_own, number, kinds_ref, relations_ref, local.at[part], remote.at[part], rel_out, out_ref,
            left, right, weights, scale,
        )


def nothing_kernel(*outs):
    pass


def add_grads(batch, halves, lives, numbers, lists_ref, grads, totals, held, sems):
    copies = [fetch_list(lists_ref, number, held[n], sems.at[n]) for n, number in enumerate(numbers)]
    for live, copy in zip(lives, copies):
        pl.when(live)(copy.start)
    for n, (live, copy) in enumerate(zip(lives, copies)):

        @pl.when(live)
        def _():
            copy.wait()
            scatter_rows(batch, halves, held[n], grads[n], totals)


def add_kernel(batch, slots, halves, pair, meta_ref, lists_ref, grads_a, grads_b, *refs):
    totals, (own, sent, sems) = refs[-3 - SUMS : -3], refs[-3:]
    if pair == 0:
        for total in totals:
            total[...] = jnp.zeros_like(total)
    live = pair < (task_count(meta_ref) - 1) >> 1
    numbers = [task_list(meta_ref, 2 * pair + part, slots)[1] for part in range(2)]
    add_grads(batch, halves, (live, live), numbers, lists_ref, (grads_a, grads_b), totals, (own, sent), sems)


def add_last_kernel(batch, slots, halves, meta_ref, lists_ref, grads_a, grads_b, *refs):
    totals, (own, sent, sems) = refs[SUMS : 2 * SUMS], refs[2 * SUMS :]
    last = (task_count(meta_ref) - 1) >> 1
    tasks = [2 * last, 2 * last + 1]
    lives = [task < task_count(meta_ref) for task in tasks]
    numbers = [jnp.where(task < 2, task * slots, task_list(meta_ref, task, slots)[1]) for task in tasks]
    add_grads(batch, halves, lives, numbers, lists_ref, (grads_a, grads_b), totals, (own, sent), sems)


def update_kernel(state_ref, rows_ref, *refs):
    totals, (table, new_state, new_rows, in_sems, out_sems) = refs[:SUMS], refs[SUMS:]
    halves, count, _ = table.shape
    width = halves * LANES
    chunk = LANES
    unroll = 8
    group = unroll * chunk

    def out_copies(number):
        rows = pl.ds(pl.multiple_of(number * group, group), group)
        return [
            pltpu.make_async_copy(
                table.at[h, rows, :], new_rows.at[rows, pl.ds(h * LANES, LANES)], out_sems.at[number, h]
            )
            for h in range(halves)
        ]

    def in_copies(number):
        rows = pl.ds(pl.multiple_of(number * group, group), group)
        return [
            pltpu.make_async_copy(
                rows_ref.at[rows, pl.ds(h * LANES, LANES)], table.at[h, rows, :], in_sems.at[number, h]
            )
            for h in range(halves)
        ]

    def begin(number, carry):
        for copy in in_copies(number):
            copy.start()
        return carry

    def update_group(number, carry):
        for copy in in_copies(number):
            copy.wait()
        for u in range(unroll):
            at = number * unroll + u
            first = pl.multiple_of(at * chunk, chunk)
            rows = pl.ds(first, chunk)
            grads = [
                sum(total[pl.ds(first * halves + h, chunk, stride=halves), :] for total in totals)
                for h in range(halves)
            ]
            squares = sum(g * g for g in grads)
            mean = jnp.sum(jnp.transpose(squares), axis=0, keepdims=True) * (1.0 / width)
            now = state_ref[pl.ds(at, 1), :] + mean
            new_state[pl.ds(at, 1), :] = now
            factor = jnp.transpose(jnp.broadcast_to(learn_rate * lax.rsqrt(now), (chunk, LANES)))
            for h in range(halves):
                table[h, rows, :] = table[h, rows, :] - grads[h] * factor
        for copy in out_copies(number):
            copy.start()
        return carry

    def finish(number, carry):
        for copy in out_copies(number):
            copy.wait()
        return carry

    lax.fori_loop(0, count // group, begin, 0)
    lax.fori_loop(0, count // group, update_group, 0)
    lax.fori_loop(0, count // group, finish, 0)


def params(mib):
    return pltpu.CompilerParams(vmem_limit_bytes=mib * MIB)


def in_vmem(array):
    return pltpu.with_memory_space_constraint(array, pltpu.VMEM)


def in_hbm(array):
    return pltpu.with_memory_space_constraint(array, pltpu.HBM)


def cost(us):
    return pl.CostEstimate(flops=0, bytes_accessed=int(us * 3.4e6), transcendentals=0)


def on_device(
    embeddings, row_state, relations, rel_state, edge_src, edge_dst, edge_rel, batch_count
):
    bit_count = lax.axis_size("dom").bit_length() - 1
    row_count, width = embeddings.shape
    slots, batch = edge_src.shape[3:]
    halves = width // LANES
    size = -(-batch // 256) * 256
    sent_size = -(-batch // 16) * 16
    list_size = -(-batch // 1024) * 1024
    pairs = slots
    sent_shape = jax.ShapeDtypeStruct((sent_size, width), bf16)
    grads_shape = jax.ShapeDtypeStruct((halves * sent_size, LANES), f32)
    rel_shape = jax.ShapeDtypeStruct(relations.shape, f32)
    table_shape = pltpu.VMEM((halves, row_count, LANES), f32)
    total_shape = pltpu.VMEM((halves * row_count, LANES), f32)
    buffer = pltpu.VMEM((halves, sent_size, LANES), f32)
    one_list = pltpu.SMEM((list_size,), jnp.int32)
    dma = pltpu.SemaphoreType.DMA
    task_scratch = [
        pltpu.VMEM((size, width), bf16),
        pltpu.VMEM((size, width), bf16),
        pltpu.VMEM((size, size), bf16),
        pltpu.VMEM((size, width), f32),
    ]
    swaps = [1 << (bit_count - 1 - number) for number in range(ROUNDS)]

    def padded(ids):
        return jnp.pad(ids, ((0, 0), (0, list_size - batch)))

    state = row_state.reshape(row_count // LANES, LANES)
    sources = [padded(edge_src[0, 0, number]) for number in range(ROUNDS)]
    is_low = jnp.stack([(lax.axis_index("dom") & swap == 0).astype(jnp.int32) for swap in swaps])
    is_low, sources = lax.optimization_barrier((is_low, sources))
    table, sent = pl.pallas_call(
        functools.partial(load_kernel, batch),
        out_shape=[table_shape, sent_shape],
        in_specs=[ANY_SPEC, HBM_SPEC],
        out_specs=[VMEM_SPEC] * 2,
        scratch_shapes=[buffer, one_list, dma, dma((halves,))],
        compiler_params=params(16),
        cost_estimate=cost(5),
        name="load_and_gather",
    )(sources[0].reshape(-1), in_hbm(embeddings))
    sent, edge_dst, edge_rel, batch_count = lax.optimization_barrier((sent, edge_dst, edge_rel, batch_count))
    got_a = from_partner(sent, "dom", swaps[0])

    rounds = []
    for number in range(ROUNDS):
        count = batch_count[0, :, number]
        tail = jnp.broadcast_to(count[:, None], (1, list_size))
        mine = jnp.concatenate([padded(edge_dst[0, 0, number]), padded(edge_rel[0, 0, number]), tail], axis=0)
        theirs = from_partner(mine, "dom", swaps[number])
        lists = jnp.concatenate([sources[number], theirs[:slots]], axis=0).reshape(-1)
        kinds = jnp.concatenate([edge_rel[0, 0, number], theirs[slots : 2 * slots, :batch]], axis=0)
        kinds = jnp.pad(kinds, ((0, 0), (0, size - batch)), constant_values=-1)
        rounds.append((lists, kinds, jnp.concatenate([count, theirs[2 * slots, :1], is_low[number : number + 1]])))
    rounds = lax.optimization_barrier(rounds)

    for number in range(ROUNDS):
        swap = swaps[number]
        lists, kinds, meta = rounds[number]

        def gather(tasks, us, table):
            return pl.pallas_call(
                functools.partial(gather_kernel, batch, slots, tasks),
                out_shape=[sent_shape] * len(tasks),
                in_specs=[SMEM_SPEC, ANY_SPEC, VMEM_SPEC],
                out_specs=[VMEM_SPEC] * len(tasks),
                scratch_shapes=[buffer] + [one_list] * len(tasks) + [dma((len(tasks),))],
                compiler_params=params(16),
                cost_estimate=cost(us / 8),
                name="gather",
            )(meta, lists, in_vmem(table))

        if number > 0:
            (sent,) = gather((0,), 2, table)
            got_a = from_partner(sent, "dom", swap)
        (second,) = gather((1,), 2, table)
        got_b = from_partner(second, "dom", swap)
        table, got_a = lax.optimization_barrier((table, got_a))
        sent = [sent, second, *gather(tuple(range(2, 2 * slots)), 6, table)]
        late, sent, got_b = lax.optimization_barrier((meta, sent, got_b))
        tasks = late[0] + late[1]
        got_a, got_b = got_b, got_a

        def run_pair(pair, relations, sent, got_a, got_b, rel_grad):
            return pl.pallas_call(
                functools.partial(pair_kernel, batch, slots, (2 * pair, 2 * pair + 1)),
                out_shape=[rel_shape, grads_shape, grads_shape],
                in_specs=[SMEM_SPEC] + [VMEM_SPEC] * 7,
                out_specs=[VMEM_SPEC] * 3,
                scratch_shapes=task_scratch,
                compiler_params=params(16),
                cost_estimate=cost(6),
                name="batches",
            )(meta, kinds, relations, sent[0], sent[1], got_a, got_b, rel_grad)

        rel_grad = jnp.zeros(relations.shape, f32)
        grads, got = [], [got_a, got_b]
        for pair in range(pairs - 1):

            def go_on(both, relations, sent, got_a, got_b, rel_grad):
                next_a = from_partner(sent[2], "dom", swap)
                next_b = from_partner(sent[3], "dom", swap) if both else sent[3]
                rel_grad, grads_a, grads_b = run_pair(pair, relations, sent, got_a, got_b, rel_grad)
                return next_a, next_b, rel_grad, grads_a, grads_b

            def skip(relations, sent, got_a, got_b, rel_grad):
                next_a, next_b, grads_a, grads_b = pl.pallas_call(
                    nothing_kernel,
                    out_shape=[sent_shape] * 2 + [grads_shape] * 2,
                    out_specs=[ANY_SPEC] * 4,
                    name="nothing",
                )()
                return next_a, next_b, rel_grad, grads_a, grads_b

            got_a, got_b, rel_grad, grads_a, grads_b = lax.switch(
                jnp.clip(tasks - 2 * pair - 2, 0, 2),
                [skip, functools.partial(go_on, False), functools.partial(go_on, True)],
                relations, sent[2 * pair : 2 * pair + 4], got_a, got_b, rel_grad,
            )
            got += [got_a, got_b]
            grads.append((grads_a, grads_b))
        rel_grad, *last_grads = pl.pallas_call(
            functools.partial(last_kernel, batch, slots, pairs),
            out_shape=[rel_shape, grads_shape, grads_shape],
            in_specs=[SMEM_SPEC] + [VMEM_SPEC] * 3 + [ANY_SPEC] * (4 * pairs),
            out_specs=[VMEM_SPEC] * 3,
            scratch_shapes=task_scratch + [pltpu.VMEM((2, *sent_shape.shape), bf16)] * 2 + [dma((2, 2))],
            compiler_params=params(16),
            cost_estimate=cost(6),
            name="last_batches",
        )(meta, kinds, relations, rel_grad, *sent, *got)

        sums = [("rep", 1 << bit) for bit in range(lax.axis_size("rep").bit_length() - 1)]
        sums += [("dom", 1 << bit) for bit in range(bit_count)]
        rel_total, totals = rel_grad, None
        for step in range(max(pairs, len(sums))):
            part = from_partner(rel_total, *sums[step]) if step < len(sums) else None
            if step < pairs:
                last = step == pairs - 1
                totals = pl.pallas_call(
                    functools.partial(add_last_kernel, batch, slots, halves)
                    if last
                    else functools.partial(add_kernel, batch, slots, halves, step),
                    out_shape=[total_shape] * SUMS,
                    in_specs=[SMEM_SPEC, ANY_SPEC] + [VMEM_SPEC] * (2 + SUMS * (step > 0)),
                    out_specs=[VMEM_SPEC] * SUMS,
                    scratch_shapes=[one_list, one_list, dma((2,))],
                    input_output_aliases={4 + n: n for n in range(SUMS)} if step > 0 else {},
                    compiler_params=params(12),
                    cost_estimate=cost(4),
                    name="add_rows",
                )(meta, lists, *(last_grads if last else grads[step]), *(map(in_vmem, totals) if step > 0 else []))
            if part is not None:
                rel_total = rel_total + part
            if step < pairs:
                rel_total, totals = lax.optimization_barrier((rel_total, totals))
        table, state, embeddings = pl.pallas_call(
            update_kernel,
            out_shape=[
                table_shape,
                jax.ShapeDtypeStruct(state.shape, f32),
                pltpu.HBM(embeddings.shape, f32),
            ],
            in_specs=[VMEM_SPEC, HBM_SPEC] + [VMEM_SPEC] * SUMS,
            out_specs=[VMEM_SPEC] * 2 + [HBM_SPEC],
            scratch_shapes=[dma((row_count // (8 * LANES), halves))] * 2,
            compiler_params=params(12),
            cost_estimate=cost(8),
            name="update",
        )(state, in_hbm(embeddings), *map(in_vmem, totals))
        rel_state = rel_state + rel_total * rel_total
        relations = relations - rel_rate * rel_total / jnp.sqrt(rel_state)
    return (embeddings, state.reshape(row_count), relations, rel_state)


def solution(mesh):
    return jax.shard_map(
        on_device,
        mesh=mesh,
        in_specs=(
            P(("dom", "rep"), None),
            P(("dom", "rep")),
            P(),
            P(),
            P("dom", "rep", None, None, None),
            P("dom", "rep", None, None, None),
            P("dom", "rep", None, None, None),
            P("dom", "rep", None),
        ),
        out_specs=(P(("dom", "rep"), None), P(("dom", "rep")), P(), P()),
        check_vma=False,
    )
```

```python
import functools

import jax
import jax.numpy as jnp
from jax import lax
from jax.experimental import pallas as pl
from jax.experimental.pallas import tpu as pltpu
from jax.sharding import PartitionSpec as P

ROUNDS = 2


learn_rate = 0.1
rel_rate = 0.1

f32 = jnp.float32
bf16 = jnp.bfloat16
MIB = 1 << 20
LANES = 128
SUMS = 3
SMEM_SPEC = pl.BlockSpec(memory_space=pltpu.SMEM)
VMEM_SPEC = pl.BlockSpec(memory_space=pltpu.VMEM)
ANY_SPEC = pl.BlockSpec(memory_space=pl.ANY)
HBM_SPEC = pl.BlockSpec(memory_space=pltpu.HBM)


def from_partner(shard, axis, distance, senders=(0, 1)):
    pairs = [(i, i ^ distance) for i in range(lax.axis_size(axis)) if (i & distance != 0) in senders]
    return lax.ppermute(shard, axis, pairs)


def unroll_of(count):
    return max(d for d in range(1, 41) if count % d == 0)


def task_list(meta_ref, task, slots):
    own, theirs, low = meta_ref[0], meta_ref[1], meta_ref[2] == 1
    if isinstance(task, int) and task < 2:
        return task == 0, task * slots
    first = jnp.where(low, own, theirs) - 1
    is_first = task - 2 < first
    number = jnp.where(is_first, task - 1, task - 1 - first)
    is_own = is_first == low
    return is_own, jnp.where(is_own, number, slots + number)


def task_count(meta_ref):
    return meta_ref[0] + meta_ref[1]


def fetch_list(lists_ref, number, list_ref, sem):
    size = list_ref.shape[0]
    return pltpu.make_async_copy(lists_ref.at[pl.ds(pl.multiple_of(number * size, size), size)], list_ref, sem)


def gather_rows(batch, list_ref, table, buffer, out_ref):
    unroll = unroll_of(batch)
    halves, size, _ = buffer.shape
    if size > batch:
        buffer[:, batch:, :] = jnp.zeros((halves, size - batch, LANES), f32)

    def step(i, carry):
        at = i * unroll
        for u in range(unroll):
            row = list_ref[at + u]
            for h in range(halves):
                buffer[h, pl.ds(at + u, 1), :] = table[h, pl.ds(row, 1), :]
        return carry

    lax.fori_loop(0, batch // unroll, step, 0)
    for h in range(halves):
        out_ref[:size, h * LANES : (h + 1) * LANES] = buffer[h].astype(bf16)


def scatter_rows(batch, halves, list_ref, grads, totals):
    unroll = unroll_of(batch)

    def step(i, carry):
        at = i * unroll
        for u in range(unroll):
            row = pl.ds(pl.multiple_of(list_ref[at + u] * halves, halves), halves)
            totals[u % SUMS][row, :] += grads[pl.ds(pl.multiple_of((at + u) * halves, halves), halves), :]
        return carry

    lax.fori_loop(0, batch // unroll, step, 0)


def load_table(rows_ref, table, sems):
    return [
        pltpu.make_async_copy(rows_ref.at[:, pl.ds(h * LANES, LANES)], table.at[h], sems.at[h])
        for h in range(table.shape[0])
    ]


def prepare_kernel(src_ref, dst_ref, rel_ref, count_ref, *refs):
    rounds, slots, batch = src_ref.shape[2:]
    for number in range(rounds):
        sources, mine = refs[number], refs[rounds + number]
        sources[:, :batch] = src_ref[0, 0, number]
        mine[:slots, :batch] = dst_ref[0, 0, number]
        mine[slots : 2 * slots, :batch] = rel_ref[0, 0, number]
        mine[2 * slots :, :] = jnp.full((1, mine.shape[1]), count_ref[0, 0, number], jnp.int32)


def load_kernel(batch, lists_ref, rows_ref, table, sent_ref, buffer, list_ref, list_sem, sems):
    copies = load_table(rows_ref, table, sems) + [fetch_list(lists_ref, 0, list_ref, list_sem)]
    for copy in copies:
        copy.start()
    for copy in copies:
        copy.wait()
    gather_rows(batch, list_ref, table, buffer, sent_ref)


def gather_kernel(batch, slots, tasks, meta_ref, lists_ref, table, *refs):
    outs, (buffer, *held, sems) = refs[: len(tasks)], refs[len(tasks) :]
    copies = [
        fetch_list(lists_ref, task_list(meta_ref, task, slots)[1], held[n], sems.at[n])
        for n, task in enumerate(tasks)
    ]
    for n, task in enumerate(tasks):
        pl.when(task < task_count(meta_ref))(copies[n].start)
    for n, task in enumerate(tasks):

        @pl.when(task < task_count(meta_ref))
        def _():
            copies[n].wait()
            gather_rows(batch, held[n], table, buffer, outs[n])


def batch_task(
    batch, live, is_own, number, kinds_ref, relations_ref, local, remote, rel_out, out_ref, left, right, weights, scale
):
    size, width = left.shape
    halves = width // LANES
    sent = local.shape[0]
    rel_count = relations_ref.shape[0]
    block = size
    inverse = 1.0 / (batch - 1)

    @pl.when(live)
    def _():
        kinds = kinds_ref[pl.ds(number, 1), :]
        full = relations_ref[...]
        high = full.astype(bf16)
        rest = full - high.astype(f32)
        middle = rest.astype(bf16)
        low = (rest - middle.astype(f32)).astype(bf16)
        kind_rows = lax.broadcasted_iota(jnp.int32, (rel_count, size), 0)
        onehot = jnp.where(kind_rows == kinds, 1.0, 0.0).astype(bf16)
        diagonal = lax.dot_general(
            jnp.concatenate([onehot, onehot, onehot], axis=0),
            jnp.concatenate([high, middle, low], axis=0),
            (((0,), (0,)), ((), ())),
            preferred_element_type=f32,
        )
        scale[...] = jnp.where(is_own, diagonal, 1.0)
        left[:sent, :] = (local[...].astype(f32) * scale[:sent, :]).astype(bf16)
        right[:sent, :] = (remote[...].astype(f32) * jnp.where(is_own, 1.0, diagonal[:sent, :])).astype(bf16)
        if size > sent:
            left[sent:, :] = jnp.zeros((size - sent, width), bf16)
            right[sent:, :] = jnp.zeros((size - sent, width), bf16)
        rel_grad = rel_out[...]
        on_diag = lax.broadcasted_iota(jnp.int32, (block, block), 0) == lax.broadcasted_iota(
            jnp.int32, (block, block), 1
        )
        for start in range(0, size, block):
            rows = pl.ds(start, block)
            scores = lax.dot_general(
                left[rows, :], right[...], (((1,), (1,)), ((), ())), preferred_element_type=f32
            )
            probs = 0.5 * jnp.tanh(0.5 * scores) + 0.5
            weights[...] = (probs * inverse).astype(bf16)
            square = probs[:, start : start + block]
            weights[:, pl.ds(start, block)] = jnp.where(on_diag, square - 1.0, square * inverse).astype(bf16)
            grads = jnp.dot(weights[...], right[...], preferred_element_type=f32)
            stop = min(start + block, sent)
            used = stop - start
            scaled = grads * scale[rows, :]
            for h in range(halves):
                out_ref[pl.ds(start * halves + h, used, stride=halves), :] = scaled[
                    :used, h * LANES : (h + 1) * LANES
                ]
            own_rows = local[start:stop, :].astype(f32)
            terms = jnp.where(is_own, grads[:used, :] * own_rows, 0.0)
            terms_high = terms.astype(bf16)
            terms_low = (terms - terms_high.astype(f32)).astype(bf16)
            kind_part = onehot[:, start:stop]
            rel_grad = (
                rel_grad
                + jnp.dot(kind_part, terms_high, preferred_element_type=f32)
                + jnp.dot(kind_part, terms_low, preferred_element_type=f32)
            )
        rel_out[...] = rel_grad


def pair_kernel(batch, slots, pair, pairs, meta_ref, kinds_ref, relations_ref, rel_in, *refs):
    mine, theirs, refs = refs[: 2 * pairs], refs[2 * pairs : 4 * pairs], refs[4 * pairs :]
    rel_out, out, left, right, weights, scale, local, remote, sems = refs
    rel_out[...] = rel_in[...]
    last = (task_count(meta_ref) - 1) >> 1 if pair is None else pair

    def copies(part, place):
        return [
            pltpu.make_async_copy(mine[2 * place + part], local.at[part], sems.at[part, 0]),
            pltpu.make_async_copy(theirs[2 * place + part], remote.at[part], sems.at[part, 1]),
        ]

    for part in range(2):
        for place in range(pairs):
            here = 2 * last + part < task_count(meta_ref)
            if pair is None:
                here = here & (last == place)

            @pl.when(here)
            def _():
                for copy in copies(part, place):
                    copy.start()

    def one_task(part, carry):
        task = 2 * last + part
        live = task < task_count(meta_ref)

        @pl.when(live)
        def _():
            pltpu.make_async_copy(mine[0], local.at[part], sems.at[part, 0]).wait()
            pltpu.make_async_copy(theirs[0], remote.at[part], sems.at[part, 1]).wait()

        is_own, number = task_list(meta_ref, task, slots)
        is_own = jnp.where(task < 2, task, jnp.where(is_own, 0, 1)) == 0
        number = jnp.where(task < 2, task * slots, number)
        batch_task(
            batch, live, is_own, number, kinds_ref, relations_ref, local.at[part], remote.at[part], rel_out,
            out.at[part], left, right, weights, scale,
        )
        return carry

    lax.fori_loop(0, 2, one_task, 0)


def nothing_kernel(*outs):
    pass


def add_grads(batch, halves, lives, numbers, lists_ref, grads, totals, held, sems):
    copies = [fetch_list(lists_ref, number, held[n], sems.at[n]) for n, number in enumerate(numbers)]
    for live, copy in zip(lives, copies):
        pl.when(live)(copy.start)
    for n, (live, copy) in enumerate(zip(lives, copies)):

        @pl.when(live)
        def _():
            copy.wait()
            scatter_rows(batch, halves, held[n], grads[n], totals)


def add_kernel(batch, slots, halves, pair, meta_ref, lists_ref, grads, *refs):
    totals, (own, sent, sems) = refs[-3 - SUMS : -3], refs[-3:]
    if pair == 0:
        for total in totals:
            total[...] = jnp.zeros_like(total)
    live = pair < (task_count(meta_ref) - 1) >> 1
    numbers = [task_list(meta_ref, 2 * pair + part, slots)[1] for part in range(2)]
    add_grads(batch, halves, (live, live), numbers, lists_ref, (grads.at[0], grads.at[1]), totals, (own, sent), sems)


def add_last_kernel(batch, slots, halves, meta_ref, lists_ref, grads, *refs):
    totals, (own, sent, sems) = refs[SUMS : 2 * SUMS], refs[2 * SUMS :]
    last = (task_count(meta_ref) - 1) >> 1
    tasks = [2 * last, 2 * last + 1]
    lives = [task < task_count(meta_ref) for task in tasks]
    numbers = [jnp.where(task < 2, task * slots, task_list(meta_ref, task, slots)[1]) for task in tasks]
    add_grads(batch, halves, lives, numbers, lists_ref, (grads.at[0], grads.at[1]), totals, (own, sent), sems)


def update_kernel(state_ref, rows_ref, *refs):
    totals, (new_state, new_rows, table, in_sems, out_sems) = refs[:SUMS], refs[SUMS:]
    halves, count, _ = table.shape
    width = halves * LANES
    chunk = LANES
    unroll = 8
    group = unroll * chunk

    def out_copies(number):
        rows = pl.ds(pl.multiple_of(number * group, group), group)
        return [
            pltpu.make_async_copy(
                table.at[h, rows, :], new_rows.at[rows, pl.ds(h * LANES, LANES)], out_sems.at[number, h]
            )
            for h in range(halves)
        ]

    def in_copies(number):
        rows = pl.ds(pl.multiple_of(number * group, group), group)
        return [
            pltpu.make_async_copy(
                rows_ref.at[rows, pl.ds(h * LANES, LANES)], table.at[h, rows, :], in_sems.at[number, h]
            )
            for h in range(halves)
        ]

    def begin(number, carry):
        for copy in in_copies(number):
            copy.start()
        return carry

    def update_group(number, carry):
        for copy in in_copies(number):
            copy.wait()
        for u in range(unroll):
            at = number * unroll + u
            first = pl.multiple_of(at * chunk, chunk)
            rows = pl.ds(first, chunk)
            grads = [
                sum(total[pl.ds(first * halves + h, chunk, stride=halves), :] for total in totals)
                for h in range(halves)
            ]
            squares = sum(g * g for g in grads)
            mean = jnp.sum(jnp.transpose(squares), axis=0, keepdims=True) * (1.0 / width)
            now = state_ref[pl.ds(at, 1), :] + mean
            new_state[pl.ds(at, 1), :] = now
            factor = jnp.transpose(jnp.broadcast_to(learn_rate * lax.rsqrt(now), (chunk, LANES)))
            for h in range(halves):
                table[h, rows, :] = table[h, rows, :] - grads[h] * factor
        for copy in out_copies(number):
            copy.start()
        return carry

    def finish(number, carry):
        for copy in out_copies(number):
            copy.wait()
        return carry

    lax.fori_loop(0, count // group, begin, 0)
    lax.fori_loop(0, count // group, update_group, 0)
    lax.fori_loop(0, count // group, finish, 0)


def params(mib):
    return pltpu.CompilerParams(vmem_limit_bytes=mib * MIB)


def in_vmem(array):
    return pltpu.with_memory_space_constraint(array, pltpu.VMEM)


def in_hbm(array):
    return pltpu.with_memory_space_constraint(array, pltpu.HBM)


def cost(us):
    return pl.CostEstimate(flops=0, bytes_accessed=int(us * 3.4e6), transcendentals=0)


def on_device(
    embeddings, row_state, relations, rel_state, edge_src, edge_dst, edge_rel, batch_count
):
    bit_count = lax.axis_size("dom").bit_length() - 1
    row_count, width = embeddings.shape
    slots, batch = edge_src.shape[3:]
    halves = width // LANES
    size = -(-batch // 256) * 256
    sent_size = -(-batch // 16) * 16
    list_size = -(-batch // 1024) * 1024
    pairs = slots
    sent_shape = jax.ShapeDtypeStruct((sent_size, width), bf16)
    grads_shape = jax.ShapeDtypeStruct((halves * sent_size, LANES), f32)
    rel_shape = jax.ShapeDtypeStruct(relations.shape, f32)
    table_shape = pltpu.VMEM((halves, row_count, LANES), f32)
    total_shape = pltpu.VMEM((halves * row_count, LANES), f32)
    buffer = pltpu.VMEM((halves, sent_size, LANES), f32)
    one_list = pltpu.SMEM((list_size,), jnp.int32)
    dma = pltpu.SemaphoreType.DMA
    task_scratch = [
        pltpu.VMEM((size, width), bf16),
        pltpu.VMEM((size, width), bf16),
        pltpu.VMEM((size, size), bf16),
        pltpu.VMEM((size, width), f32),
    ]
    swaps = [1 << (bit_count - 1 - number) for number in range(ROUNDS)]

    state = row_state.reshape(row_count // LANES, LANES)
    list_shape = jax.ShapeDtypeStruct((slots, list_size), jnp.int32)
    prepared = pl.pallas_call(
        prepare_kernel,
        out_shape=[list_shape] * ROUNDS + [jax.ShapeDtypeStruct((2 * slots + 1, list_size), jnp.int32)] * ROUNDS,
        in_specs=[VMEM_SPEC] * 3 + [SMEM_SPEC],
        out_specs=[VMEM_SPEC] * (2 * ROUNDS),
        compiler_params=params(16),
        cost_estimate=cost(1),
        name="prepare",
    )(in_hbm(edge_src), in_hbm(edge_dst), in_hbm(edge_rel), batch_count)
    sources, mine = prepared[:ROUNDS], prepared[ROUNDS:]
    theirs = [from_partner(mine[number], "dom", swaps[number]) for number in range(ROUNDS)]
    is_low = jnp.stack([(lax.axis_index("dom") & swap == 0).astype(jnp.int32) for swap in swaps])
    is_low, sources = lax.optimization_barrier((is_low, sources))
    table, sent = pl.pallas_call(
        functools.partial(load_kernel, batch),
        out_shape=[table_shape, sent_shape],
        in_specs=[ANY_SPEC, HBM_SPEC],
        out_specs=[VMEM_SPEC] * 2,
        scratch_shapes=[buffer, one_list, dma, dma((halves,))],
        compiler_params=params(16),
        cost_estimate=cost(5),
        name="load_and_gather",
    )(sources[0].reshape(-1), in_hbm(embeddings))
    got_a = from_partner(sent, "dom", swaps[0])

    rounds = []
    for number in range(ROUNDS):
        count = batch_count[0, :, number]
        their = theirs[number]
        lists = jnp.concatenate([sources[number], their[:slots]], axis=0).reshape(-1)
        kinds = jnp.concatenate([edge_rel[0, 0, number], their[slots : 2 * slots, :batch]], axis=0)
        kinds = jnp.pad(kinds, ((0, 0), (0, size - batch)), constant_values=-1)
        rounds.append((lists, kinds, jnp.concatenate([count, their[2 * slots, :1], is_low[number : number + 1]])))
    rounds = lax.optimization_barrier(rounds)

    for number in range(ROUNDS):
        swap = swaps[number]
        lists, kinds, meta = rounds[number]

        def gather(tasks, us, table):
            return pl.pallas_call(
                functools.partial(gather_kernel, batch, slots, tasks),
                out_shape=[sent_shape] * len(tasks),
                in_specs=[SMEM_SPEC, ANY_SPEC, VMEM_SPEC],
                out_specs=[VMEM_SPEC] * len(tasks),
                scratch_shapes=[buffer] + [one_list] * len(tasks) + [dma((len(tasks),))],
                compiler_params=params(16),
                cost_estimate=cost(us / 8),
                name="gather",
            )(meta, lists, in_vmem(table))

        if number > 0:
            (sent,) = gather((0,), 2, table)
            got_a = from_partner(sent, "dom", swap)
        (second,) = gather((1,), 2, table)
        got_b = from_partner(second, "dom", swap)
        if number == 0:
            table, got_a = lax.optimization_barrier((table, got_a))
        sent = [sent, second, *gather(tuple(range(2, 2 * slots)), 6, table)]
        late, sent, got_b = lax.optimization_barrier((meta, sent, got_b))
        tasks = late[0] + late[1]
        got_a, got_b = got_b, got_a

        both_grads = jax.ShapeDtypeStruct((2, *grads_shape.shape), f32)

        def run_pair(pair, relations, sent, got, rel_grad):
            return pl.pallas_call(
                functools.partial(pair_kernel, batch, slots, pair, len(sent) // 2),
                out_shape=[rel_shape, both_grads],
                in_specs=[SMEM_SPEC] + [VMEM_SPEC] * 3 + [ANY_SPEC] * (2 * len(sent)),
                out_specs=[VMEM_SPEC] * 2,
                scratch_shapes=task_scratch + [pltpu.VMEM((2, *sent_shape.shape), bf16)] * 2 + [dma((2, 2))],
                compiler_params=params(16),
                cost_estimate=cost(6),
                name="batches",
            )(meta, kinds, relations, rel_grad, *sent, *got)

        def nothing(*shapes):
            return pl.pallas_call(
                nothing_kernel, out_shape=list(shapes), out_specs=[ANY_SPEC] * len(shapes), name="nothing"
            )()

        rel_grad = jnp.zeros(relations.shape, f32)
        grads, got = [], [got_a, got_b]
        for pair in range(pairs - 1):

            def go_on(tasks, relations, sent, got, rel_grad):
                next_a = from_partner(sent[2], "dom", swap)
                rel_grad, grads = run_pair(pair, relations, sent[:2], got, rel_grad)
                second, rel_grad = lax.optimization_barrier((sent[3], rel_grad))
                next_b = lax.cond(
                    tasks > 2 * pair + 3,
                    lambda second: from_partner(second, "dom", swap),
                    lambda second: nothing(sent_shape)[0],
                    second,
                )
                return next_a, next_b, rel_grad, grads

            def skip(tasks, relations, sent, got, rel_grad):
                next_a, next_b, grads = nothing(sent_shape, sent_shape, both_grads)
                return next_a, next_b, rel_grad, grads

            *next_got, rel_grad, part = lax.cond(
                tasks > 2 * pair + 2, go_on, skip, tasks, relations, sent[2 * pair : 2 * pair + 4], got[-2:], rel_grad
            )
            got += next_got
            grads.append(part)
        rel_grad, last_grads = run_pair(None, relations, sent, got, rel_grad)
        grads.append(last_grads)

        sums = [("dom", 1 << bit) for bit in reversed(range(bit_count))]
        sums += [("rep", 1 << bit) for bit in reversed(range(lax.axis_size("rep").bit_length() - 1))]
        rel_total, totals = rel_grad, None
        for step in range(max(pairs, len(sums))):
            part = from_partner(rel_total, *sums[step]) if step < len(sums) else None
            if step < pairs:
                last = step == pairs - 1
                totals = pl.pallas_call(
                    functools.partial(add_last_kernel, batch, slots, halves)
                    if last
                    else functools.partial(add_kernel, batch, slots, halves, step),
                    out_shape=[total_shape] * SUMS,
                    in_specs=[SMEM_SPEC, ANY_SPEC] + [VMEM_SPEC] * (1 + SUMS * (step > 0)),
                    out_specs=[VMEM_SPEC] * SUMS,
                    scratch_shapes=[one_list, one_list, dma((2,))],
                    input_output_aliases={3 + n: n for n in range(SUMS)} if step > 0 else {},
                    compiler_params=params(12),
                    cost_estimate=cost(4),
                    name="add_rows",
                )(meta, lists, grads[step], *(map(in_vmem, totals) if step > 0 else []))
            if part is not None:
                rel_total = rel_total + part
            if step < pairs:
                rel_total, totals = lax.optimization_barrier((rel_total, totals))
        more = number + 1 < ROUNDS
        state, embeddings, *tables = pl.pallas_call(
            update_kernel,
            out_shape=[jax.ShapeDtypeStruct(state.shape, f32), pltpu.HBM(embeddings.shape, f32)]
            + [table_shape] * more,
            in_specs=[VMEM_SPEC, HBM_SPEC] + [VMEM_SPEC] * SUMS,
            out_specs=[VMEM_SPEC, HBM_SPEC] + [VMEM_SPEC] * more,
            scratch_shapes=[table_shape] * (not more) + [dma((row_count // (8 * LANES), halves))] * 2,
            compiler_params=params(12),
            cost_estimate=cost(8),
            name="update",
        )(state, in_hbm(embeddings), *map(in_vmem, totals))
        table = tables[0] if more else None
        rel_state = rel_state + rel_total * rel_total
        relations = relations - rel_rate * rel_total / jnp.sqrt(rel_state)
    return (embeddings, state.reshape(row_count), relations, rel_state)


def solution(mesh):
    return jax.shard_map(
        on_device,
        mesh=mesh,
        in_specs=(
            P(("dom", "rep"), None),
            P(("dom", "rep")),
            P(),
            P(),
            P("dom", "rep", None, None, None),
            P("dom", "rep", None, None, None),
            P("dom", "rep", None, None, None),
            P("dom", "rep", None),
        ),
        out_specs=(P(("dom", "rep"), None), P(("dom", "rep")), P(), P()),
        check_vma=False,
    )
```

```python
import functools

import jax
import jax.numpy as jnp
from jax import lax
from jax.experimental import pallas as pl
from jax.experimental.pallas import tpu as pltpu
from jax.sharding import PartitionSpec as P

ROUNDS = 2


learn_rate = 0.1
rel_rate = 0.1

f32 = jnp.float32
bf16 = jnp.bfloat16
MIB = 1 << 20
LANES = 128
SUMS = 3
SPARE = 8
SMEM_SPEC = pl.BlockSpec(memory_space=pltpu.SMEM)
VMEM_SPEC = pl.BlockSpec(memory_space=pltpu.VMEM)
ANY_SPEC = pl.BlockSpec(memory_space=pl.ANY)
HBM_SPEC = pl.BlockSpec(memory_space=pltpu.HBM)


def from_partner(shard, axis, distance, senders=(0, 1)):
    pairs = [(i, i ^ distance) for i in range(lax.axis_size(axis)) if (i & distance != 0) in senders]
    return lax.ppermute(shard, axis, pairs)


def unroll_of(count):
    return max(d for d in range(1, 41) if count % d == 0)


def task_list(meta_ref, task, slots):
    own, theirs, low = meta_ref[0], meta_ref[1], meta_ref[2] == 1
    if isinstance(task, int) and task < 2:
        return task == 0, task * slots
    first = jnp.where(low, own, theirs) - 1
    is_first = task - 2 < first
    number = jnp.where(is_first, task - 1, task - 1 - first)
    is_own = is_first == low
    return is_own, jnp.where(is_own, number, slots + number)


def task_count(meta_ref):
    return meta_ref[0] + meta_ref[1]


def fetch_list(lists_ref, number, list_ref, sem):
    size = list_ref.shape[0]
    return pltpu.make_async_copy(lists_ref.at[pl.ds(pl.multiple_of(number * size, size), size)], list_ref, sem)


def gather_rows(batch, list_ref, table, buffer, out_ref):
    unroll = unroll_of(batch)
    halves, size = buffer.shape[0], out_ref.shape[0]
    if size > batch:
        buffer[:, batch:size, :] = jnp.zeros((halves, size - batch, LANES), f32)

    def step(i, carry):
        at = i * unroll
        for u in range(unroll):
            row = list_ref[at + u]
            for h in range(halves):
                buffer[h, pl.ds(at + u, 1), :] = table[h, pl.ds(row, 1), :]
        return carry

    lax.fori_loop(0, batch // unroll, step, 0)
    for h in range(halves):
        out_ref[:, h * LANES : (h + 1) * LANES] = buffer[h, :size, :].astype(bf16)


def scatter_rows(batch, halves, list_ref, grads, totals):
    unroll = unroll_of(batch)

    def step(i, carry):
        at = i * unroll
        for u in range(unroll):
            row = pl.ds(pl.multiple_of(list_ref[at + u] * halves, halves), halves)
            totals[u % SUMS][row, :] += grads[pl.ds(pl.multiple_of((at + u) * halves, halves), halves), :]
        return carry

    lax.fori_loop(0, batch // unroll, step, 0)


def load_table(rows_ref, table, sems):
    return [
        pltpu.make_async_copy(
            rows_ref.at[:, pl.ds(h * LANES, LANES)], table.at[h, pl.ds(0, rows_ref.shape[0]), :], sems.at[h]
        )
        for h in range(table.shape[0])
    ]


def prepare_kernel(src_ref, dst_ref, rel_ref, count_ref, *refs):
    rounds, slots, batch = src_ref.shape[2:]
    for number in range(rounds):
        sources, mine = refs[number], refs[rounds + number]
        sources[:, :batch] = src_ref[0, 0, number]
        mine[:slots, :batch] = dst_ref[0, 0, number]
        mine[slots : 2 * slots, :batch] = rel_ref[0, 0, number]
        mine[2 * slots :, :] = jnp.full((1, mine.shape[1]), count_ref[0, 0, number], jnp.int32)


def load_kernel(batch, lists_ref, rows_ref, table, sent_ref, buffer, list_ref, list_sem, sems):
    copies = load_table(rows_ref, table, sems) + [fetch_list(lists_ref, 0, list_ref, list_sem)]
    for copy in copies:
        copy.start()
    for copy in copies:
        copy.wait()
    gather_rows(batch, list_ref, table, buffer, sent_ref)


def gather_kernel(batch, slots, tasks, meta_ref, lists_ref, table, *refs):
    outs, (buffer, *held, sems) = refs[: len(tasks)], refs[len(tasks) :]
    copies = [
        fetch_list(lists_ref, task_list(meta_ref, task, slots)[1], held[n], sems.at[n])
        for n, task in enumerate(tasks)
    ]
    for n, task in enumerate(tasks):
        pl.when(task < task_count(meta_ref))(copies[n].start)
    for n, task in enumerate(tasks):

        @pl.when(task < task_count(meta_ref))
        def _():
            copies[n].wait()
            gather_rows(batch, held[n], table, buffer, outs[n])


def batch_task(
    batch, live, is_own, number, arrive, kinds_ref, relations_ref, local, remote, rel_out, out_ref,
    left, right, weights, scale,
):
    size, width = left.shape
    halves = width // LANES
    sent = local.shape[0]
    rel_count = relations_ref.shape[0]
    inverse = 1.0 / (batch - 1)

    @pl.when(live)
    def _():
        kinds = kinds_ref[pl.ds(number, 1), :]
        full = relations_ref[...]
        high = full.astype(bf16)
        rest = full - high.astype(f32)
        middle = rest.astype(bf16)
        low = (rest - middle.astype(f32)).astype(bf16)
        kind_rows = lax.broadcasted_iota(jnp.int32, (rel_count, size), 0)
        onehot = jnp.where(kind_rows == kinds, 1.0, 0.0).astype(bf16)
        diagonal = lax.dot_general(
            jnp.concatenate([onehot, onehot, onehot], axis=0),
            jnp.concatenate([high, middle, low], axis=0),
            (((0,), (0,)), ((), ())),
            preferred_element_type=f32,
        )
        scale[...] = jnp.where(is_own, diagonal, 1.0)
        arrive()
        left[:sent, :] = (0.5 * (local[...].astype(f32) * scale[:sent, :]).astype(bf16).astype(f32)).astype(bf16)
        right[:sent, :] = (remote[...].astype(f32) * jnp.where(is_own, 1.0, diagonal[:sent, :])).astype(bf16)
        if size > sent:
            left[sent:, :] = jnp.zeros((size - sent, width), bf16)
            right[sent:, :] = jnp.zeros((size - sent, width), bf16)
        bends = jnp.tanh(
            lax.dot_general(left[...], right[...], (((1,), (1,)), ((), ())), preferred_element_type=f32)
        )
        weights[...] = (bends * (0.5 * inverse) + 0.5 * inverse).astype(bf16)
        side = LANES
        on_diag = lax.broadcasted_iota(jnp.int32, (side, side), 0) == lax.broadcasted_iota(
            jnp.int32, (side, side), 1
        )
        for start in range(0, size, side):
            probs = 0.5 * bends[start : start + side, start : start + side] + 0.5
            square = jnp.where(on_diag, probs - 1.0, probs * inverse).astype(bf16)
            weights[pl.ds(start, side), pl.ds(start, side)] = square
        grads = jnp.dot(weights[...], right[...], preferred_element_type=f32)
        scaled = grads * scale[...]
        for h in range(halves):
            out_ref[pl.ds(h, sent, stride=halves), :] = scaled[:sent, h * LANES : (h + 1) * LANES]
        terms = jnp.where(is_own, grads[:sent, :] * local[...].astype(f32), 0.0)
        terms_high = terms.astype(bf16)
        terms_low = (terms - terms_high.astype(f32)).astype(bf16)
        kind_part = onehot[:, :sent]
        rel_grad = (
            rel_out[...]
            + jnp.dot(kind_part, terms_high, preferred_element_type=f32)
            + jnp.dot(kind_part, terms_low, preferred_element_type=f32)
        )
        rel_out[...] = rel_grad


def pair_kernel(batch, slots, pair, pairs, meta_ref, kinds_ref, relations_ref, rel_in, *refs):
    mine, theirs, refs = refs[: 2 * pairs], refs[2 * pairs : 4 * pairs], refs[4 * pairs :]
    rel_out, out, left, right, weights, scale, local, remote, sems = refs
    rel_out[...] = rel_in[...]
    last = (task_count(meta_ref) - 1) >> 1 if pair is None else pair

    def copies(part, place):
        return [
            pltpu.make_async_copy(mine[2 * place + part], local.at[part], sems.at[part, 0]),
            pltpu.make_async_copy(theirs[2 * place + part], remote.at[part], sems.at[part, 1]),
        ]

    for part in range(2):
        for place in range(pairs):
            here = 2 * last + part < task_count(meta_ref)
            if pair is None:
                here = here & (last == place)

            @pl.when(here)
            def _():
                for copy in copies(part, place):
                    copy.start()

    def one_task(part, carry):
        task = 2 * last + part
        live = task < task_count(meta_ref)

        def arrive():
            pltpu.make_async_copy(mine[0], local.at[part], sems.at[part, 0]).wait()
            pltpu.make_async_copy(theirs[0], remote.at[part], sems.at[part, 1]).wait()

        is_own, number = task_list(meta_ref, task, slots)
        is_own = jnp.where(task < 2, task, jnp.where(is_own, 0, 1)) == 0
        number = jnp.where(task < 2, task * slots, number)
        batch_task(
            batch, live, is_own, number, arrive, kinds_ref, relations_ref, local.at[part], remote.at[part], rel_out,
            out.at[part], left, right, weights, scale,
        )
        return carry

    lax.fori_loop(0, 2, one_task, 0)


def nothing_kernel(*outs):
    pass


def add_grads(batch, halves, lives, numbers, lists_ref, grads, totals, held, sems):
    copies = [fetch_list(lists_ref, number, held[n], sems.at[n]) for n, number in enumerate(numbers)]
    for live, copy in zip(lives, copies):
        pl.when(live)(copy.start)
    for n, (live, copy) in enumerate(zip(lives, copies)):

        @pl.when(live)
        def _():
            copy.wait()
            scatter_rows(batch, halves, held[n], grads[n], totals)


def add_kernel(batch, slots, halves, pair, meta_ref, lists_ref, grads, *refs):
    totals, (own, sent, sems) = refs[-3 - SUMS : -3], refs[-3:]
    if pair == 0:
        for total in totals:
            total[...] = jnp.zeros_like(total)
    live = pair < (task_count(meta_ref) - 1) >> 1
    numbers = [task_list(meta_ref, 2 * pair + part, slots)[1] for part in range(2)]
    add_grads(batch, halves, (live, live), numbers, lists_ref, (grads.at[0], grads.at[1]), totals, (own, sent), sems)


def add_last_kernel(batch, slots, halves, meta_ref, lists_ref, grads, *refs):
    totals, (own, sent, sems) = refs[SUMS : 2 * SUMS], refs[2 * SUMS :]
    last = (task_count(meta_ref) - 1) >> 1
    tasks = [2 * last, 2 * last + 1]
    lives = [task < task_count(meta_ref) for task in tasks]
    numbers = [jnp.where(task < 2, task * slots, task_list(meta_ref, task, slots)[1]) for task in tasks]
    add_grads(batch, halves, lives, numbers, lists_ref, (grads.at[0], grads.at[1]), totals, (own, sent), sems)


def update_kernel(state_ref, rows_ref, *refs):
    totals, (new_state, new_rows, table, in_sems, out_sems) = refs[:SUMS], refs[SUMS:]
    halves, count = table.shape[0], rows_ref.shape[0]
    width = halves * LANES
    chunk = LANES
    unroll = 8
    group = unroll * chunk

    def out_copies(number):
        rows = pl.ds(pl.multiple_of(number * group, group), group)
        return [
            pltpu.make_async_copy(
                table.at[h, rows, :], new_rows.at[rows, pl.ds(h * LANES, LANES)], out_sems.at[number, h]
            )
            for h in range(halves)
        ]

    def in_copies(number):
        rows = pl.ds(pl.multiple_of(number * group, group), group)
        return [
            pltpu.make_async_copy(
                rows_ref.at[rows, pl.ds(h * LANES, LANES)], table.at[h, rows, :], in_sems.at[number, h]
            )
            for h in range(halves)
        ]

    def begin(number, carry):
        for copy in in_copies(number):
            copy.start()
        return carry

    def update_group(number, carry):
        for copy in in_copies(number):
            copy.wait()
        for u in range(unroll):
            at = number * unroll + u
            first = pl.multiple_of(at * chunk, chunk)
            rows = pl.ds(first, chunk)
            grads = [
                sum(total[pl.ds(first * halves + h, chunk, stride=halves), :] for total in totals)
                for h in range(halves)
            ]
            squares = sum(g * g for g in grads)
            mean = jnp.sum(jnp.transpose(squares), axis=0, keepdims=True) * (1.0 / width)
            now = state_ref[pl.ds(at, 1), :] + mean
            new_state[pl.ds(at, 1), :] = now
            factor = jnp.transpose(jnp.broadcast_to(learn_rate * lax.rsqrt(now), (chunk, LANES)))
            for h in range(halves):
                table[h, rows, :] = table[h, rows, :] - grads[h] * factor
        for copy in out_copies(number):
            copy.start()
        return carry

    def finish(number, carry):
        for copy in out_copies(number):
            copy.wait()
        return carry

    lax.fori_loop(0, count // group, begin, 0)
    lax.fori_loop(0, count // group, update_group, 0)
    lax.fori_loop(0, count // group, finish, 0)


def update_relations(relations, rel_state, rel_total):
    rel_state = rel_state + rel_total * rel_total
    return relations - rel_rate * rel_total / jnp.sqrt(rel_state), rel_state


def params(mib):
    return pltpu.CompilerParams(vmem_limit_bytes=mib * MIB)


def in_vmem(array):
    return pltpu.with_memory_space_constraint(array, pltpu.VMEM)


def in_hbm(array):
    return pltpu.with_memory_space_constraint(array, pltpu.HBM)


def cost(us):
    return pl.CostEstimate(flops=0, bytes_accessed=int(us * 3.4e6), transcendentals=0)


def on_device(
    embeddings, row_state, relations, rel_state, edge_src, edge_dst, edge_rel, batch_count
):
    bit_count = lax.axis_size("dom").bit_length() - 1
    row_count, width = embeddings.shape
    slots, batch = edge_src.shape[3:]
    halves = width // LANES
    size = -(-batch // 256) * 256
    sent_size = -(-batch // 16) * 16
    list_size = -(-batch // 1024) * 1024
    pairs = slots
    sent_shape = jax.ShapeDtypeStruct((sent_size, width), bf16)
    grads_shape = jax.ShapeDtypeStruct((halves * sent_size + SPARE, LANES), f32)
    rel_shape = jax.ShapeDtypeStruct(relations.shape, f32)
    table_shape = pltpu.VMEM((halves, row_count + SPARE, LANES), f32)
    total_shape = pltpu.VMEM((halves * row_count + SPARE, LANES), f32)
    buffer = pltpu.VMEM((halves, sent_size + SPARE, LANES), f32)
    one_list = pltpu.SMEM((list_size,), jnp.int32)
    dma = pltpu.SemaphoreType.DMA
    task_scratch = [
        pltpu.VMEM((size, width), bf16),
        pltpu.VMEM((size, width), bf16),
        pltpu.VMEM((size, size), bf16),
        pltpu.VMEM((size, width), f32),
    ]
    swaps = [1 << (bit_count - 1 - number) for number in range(ROUNDS)]

    state = row_state.reshape(row_count // LANES, LANES)
    list_shape = jax.ShapeDtypeStruct((slots, list_size), jnp.int32)
    prepared = pl.pallas_call(
        prepare_kernel,
        out_shape=[list_shape] * ROUNDS + [jax.ShapeDtypeStruct((2 * slots + 1, list_size), jnp.int32)] * ROUNDS,
        in_specs=[VMEM_SPEC] * 3 + [SMEM_SPEC],
        out_specs=[VMEM_SPEC] * (2 * ROUNDS),
        compiler_params=params(16),
        cost_estimate=cost(1),
        name="prepare",
    )(in_hbm(edge_src), in_hbm(edge_dst), in_hbm(edge_rel), batch_count)
    sources, mine = prepared[:ROUNDS], prepared[ROUNDS:]
    theirs = [from_partner(mine[number], "dom", swaps[number]) for number in range(ROUNDS)]
    is_low = jnp.stack([(lax.axis_index("dom") & swap == 0).astype(jnp.int32) for swap in swaps])
    is_low, sources = lax.optimization_barrier((is_low, sources))
    table, sent = pl.pallas_call(
        functools.partial(load_kernel, batch),
        out_shape=[table_shape, sent_shape],
        in_specs=[ANY_SPEC, HBM_SPEC],
        out_specs=[VMEM_SPEC] * 2,
        scratch_shapes=[buffer, one_list, dma, dma((halves,))],
        compiler_params=params(16),
        cost_estimate=cost(5),
        name="load_and_gather",
    )(sources[0].reshape(-1), in_hbm(embeddings))
    got_a = from_partner(sent, "dom", swaps[0])

    rounds = []
    for number in range(ROUNDS):
        count = batch_count[0, :, number]
        their = theirs[number]
        lists = jnp.concatenate([sources[number], their[:slots]], axis=0).reshape(-1)
        kinds = jnp.concatenate([edge_rel[0, 0, number], their[slots : 2 * slots, :batch]], axis=0)
        kinds = jnp.pad(kinds, ((0, 0), (0, size - batch)), constant_values=-1)
        rounds.append((lists, kinds, jnp.concatenate([count, their[2 * slots, :1], is_low[number : number + 1]])))
    rounds = lax.optimization_barrier(rounds)

    for number in range(ROUNDS):
        swap = swaps[number]
        lists, kinds, meta = rounds[number]

        def gather(tasks, us, table):
            return pl.pallas_call(
                functools.partial(gather_kernel, batch, slots, tasks),
                out_shape=[sent_shape] * len(tasks),
                in_specs=[SMEM_SPEC, ANY_SPEC, VMEM_SPEC],
                out_specs=[VMEM_SPEC] * len(tasks),
                scratch_shapes=[buffer] + [one_list] * len(tasks) + [dma((len(tasks),))],
                compiler_params=params(16),
                cost_estimate=cost(us / 8),
                name="gather",
            )(meta, lists, in_vmem(table))

        if number > 0:
            (sent,) = gather((0,), 2, table)
            got_a = from_partner(sent, "dom", swap)
        (second,) = gather((1,), 2, table)
        got_b = from_partner(second, "dom", swap)
        if number == 0:
            table, got_a = lax.optimization_barrier((table, got_a))
        sent = [sent, second, *gather(tuple(range(2, 2 * slots)), 6, table)]
        if number > 0:
            rel_total, sent = lax.optimization_barrier((rel_total, sent))
            rel_total = rel_total + from_partner(rel_total, *sums[-1])
            relations, rel_state = update_relations(relations, rel_state, rel_total)
        late, sent, got_b = lax.optimization_barrier((meta, sent, got_b))
        tasks = late[0] + late[1]
        got_a, got_b = got_b, got_a

        both_grads = jax.ShapeDtypeStruct((2, *grads_shape.shape), f32)

        def run_pair(pair, relations, sent, got, rel_grad):
            return pl.pallas_call(
                functools.partial(pair_kernel, batch, slots, pair, len(sent) // 2),
                out_shape=[rel_shape, both_grads],
                in_specs=[SMEM_SPEC] + [VMEM_SPEC] * 3 + [ANY_SPEC] * (2 * len(sent)),
                out_specs=[VMEM_SPEC] * 2,
                scratch_shapes=task_scratch + [pltpu.VMEM((2, *sent_shape.shape), bf16)] * 2 + [dma((2, 2))],
                compiler_params=params(16),
                cost_estimate=cost(6),
                name="batches",
            )(meta, kinds, relations, rel_grad, *sent, *got)

        def nothing(*shapes):
            return pl.pallas_call(
                nothing_kernel, out_shape=list(shapes), out_specs=[ANY_SPEC] * len(shapes), name="nothing"
            )()

        rel_grad = jnp.zeros(relations.shape, f32)
        grads, got = [], [got_a, got_b]
        for pair in range(pairs - 1):

            def go_on(tasks, relations, sent, got, rel_grad):
                next_a = from_partner(sent[2], "dom", swap)
                rel_grad, grads = run_pair(pair, relations, sent[:2], got, rel_grad)
                second, rel_grad = lax.optimization_barrier((sent[3], rel_grad))
                next_b = lax.cond(
                    tasks > 2 * pair + 3,
                    lambda second: from_partner(second, "dom", swap),
                    lambda second: nothing(sent_shape)[0],
                    second,
                )
                return next_a, next_b, rel_grad, grads

            def skip(tasks, relations, sent, got, rel_grad):
                next_a, next_b, grads = nothing(sent_shape, sent_shape, both_grads)
                return next_a, next_b, rel_grad, grads

            *next_got, rel_grad, part = lax.cond(
                tasks > 2 * pair + 2, go_on, skip, tasks, relations, sent[2 * pair : 2 * pair + 4], got[-2:], rel_grad
            )
            got += next_got
            grads.append(part)
        rel_grad, last_grads = run_pair(None, relations, sent, got, rel_grad)
        grads.append(last_grads)

        sums = [("dom", 1 << bit) for bit in reversed(range(bit_count))]
        sums += [("rep", 1 << bit) for bit in reversed(range(lax.axis_size("rep").bit_length() - 1))]
        rel_total, totals = rel_grad, None
        for step in range(max(pairs, len(sums))):
            part = from_partner(rel_total, *sums[step]) if step < len(sums) - (number + 1 < ROUNDS) else None
            if step < pairs:
                last = step == pairs - 1
                totals = pl.pallas_call(
                    functools.partial(add_last_kernel, batch, slots, halves)
                    if last
                    else functools.partial(add_kernel, batch, slots, halves, step),
                    out_shape=[total_shape] * SUMS,
                    in_specs=[SMEM_SPEC, ANY_SPEC] + [VMEM_SPEC] * (1 + SUMS * (step > 0)),
                    out_specs=[VMEM_SPEC] * SUMS,
                    scratch_shapes=[one_list, one_list, dma((2,))],
                    input_output_aliases={3 + n: n for n in range(SUMS)} if step > 0 else {},
                    compiler_params=params(12),
                    cost_estimate=cost(4),
                    name="add_rows",
                )(meta, lists, grads[step], *(map(in_vmem, totals) if step > 0 else []))
            if part is not None:
                rel_total = rel_total + part
            if step < pairs:
                rel_total, totals = lax.optimization_barrier((rel_total, totals))
        more = number + 1 < ROUNDS
        state, embeddings, *tables = pl.pallas_call(
            update_kernel,
            out_shape=[jax.ShapeDtypeStruct(state.shape, f32), pltpu.HBM(embeddings.shape, f32)]
            + [table_shape] * more,
            in_specs=[VMEM_SPEC, HBM_SPEC] + [VMEM_SPEC] * SUMS,
            out_specs=[VMEM_SPEC, HBM_SPEC] + [VMEM_SPEC] * more,
            scratch_shapes=[table_shape] * (not more) + [dma((row_count // (8 * LANES), halves))] * 2,
            compiler_params=params(12),
            cost_estimate=cost(8),
            name="update",
        )(state, in_hbm(embeddings), *map(in_vmem, totals))
        table = tables[0] if more else None
        if not more:
            relations, rel_state = update_relations(relations, rel_state, rel_total)
    return (embeddings, state.reshape(row_count), relations, rel_state)


def solution(mesh):
    return jax.shard_map(
        on_device,
        mesh=mesh,
        in_specs=(
            P(("dom", "rep"), None),
            P(("dom", "rep")),
            P(),
            P(),
            P("dom", "rep", None, None, None),
            P("dom", "rep", None, None, None),
            P("dom", "rep", None, None, None),
            P("dom", "rep", None),
        ),
        out_specs=(P(("dom", "rep"), None), P(("dom", "rep")), P(), P()),
        check_vma=False,
    )
```

```python
import functools

import jax
import jax.numpy as jnp
from jax import lax
from jax.experimental import pallas as pl
from jax.experimental.pallas import tpu as pltpu
from jax.sharding import PartitionSpec as P

ROUNDS = 2


learn_rate = 0.1
rel_rate = 0.1

f32 = jnp.float32
bf16 = jnp.bfloat16
MIB = 1 << 20
LANES = 128
SUMS = 3
SPARE = 8
SMEM_SPEC = pl.BlockSpec(memory_space=pltpu.SMEM)
VMEM_SPEC = pl.BlockSpec(memory_space=pltpu.VMEM)
ANY_SPEC = pl.BlockSpec(memory_space=pl.ANY)
HBM_SPEC = pl.BlockSpec(memory_space=pltpu.HBM)


def from_partner(shard, axis, distance, senders=(0, 1)):
    pairs = [(i, i ^ distance) for i in range(lax.axis_size(axis)) if (i & distance != 0) in senders]
    return lax.ppermute(shard, axis, pairs)


def unroll_of(count):
    return max(d for d in range(1, 41) if count % d == 0)


def task_list(meta_ref, task, slots):
    own, theirs, low = meta_ref[0], meta_ref[1], meta_ref[2] == 1
    if isinstance(task, int) and task < 2:
        return task == 0, task * slots
    first = jnp.where(low, own, theirs) - 1
    is_first = task - 2 < first
    number = jnp.where(is_first, task - 1, task - 1 - first)
    is_own = is_first == low
    return is_own, jnp.where(is_own, number, slots + number)


def task_count(meta_ref):
    return meta_ref[0] + meta_ref[1]


def fetch_list(lists_ref, number, list_ref, sem):
    size = list_ref.shape[0]
    return pltpu.make_async_copy(lists_ref.at[pl.ds(pl.multiple_of(number * size, size), size)], list_ref, sem)


def gather_rows(batch, list_ref, table, buffer, out_ref):
    unroll = unroll_of(batch)
    halves, size = buffer.shape[0], out_ref.shape[0]
    if size > batch:
        buffer[:, batch:size, :] = jnp.zeros((halves, size - batch, LANES), f32)

    def step(i, carry):
        at = i * unroll
        for u in range(unroll):
            row = list_ref[at + u]
            for h in range(halves):
                buffer[h, pl.ds(at + u, 1), :] = table[h, pl.ds(row, 1), :]
        return carry

    lax.fori_loop(0, batch // unroll, step, 0)
    for h in range(halves):
        out_ref[:, h * LANES : (h + 1) * LANES] = buffer[h, :size, :].astype(bf16)


def scatter_rows(batch, halves, list_ref, grads, totals):
    unroll = unroll_of(batch)

    def step(i, carry):
        at = i * unroll
        for u in range(unroll):
            row = pl.ds(pl.multiple_of(list_ref[at + u] * halves, halves), halves)
            totals[u % SUMS][row, :] += grads[pl.ds(pl.multiple_of((at + u) * halves, halves), halves), :]
        return carry

    lax.fori_loop(0, batch // unroll, step, 0)


def load_table(rows_ref, table, sems):
    return [
        pltpu.make_async_copy(
            rows_ref.at[:, pl.ds(h * LANES, LANES)], table.at[h, pl.ds(0, rows_ref.shape[0]), :], sems.at[h]
        )
        for h in range(table.shape[0])
    ]


def prepare_kernel(src_ref, dst_ref, rel_ref, count_ref, *refs):
    rounds, slots, batch = src_ref.shape[2:]
    for number in range(rounds):
        sources, mine = refs[number], refs[rounds + number]
        sources[:, :batch] = src_ref[0, 0, number]
        mine[:slots, :batch] = dst_ref[0, 0, number]
        mine[slots : 2 * slots, :batch] = rel_ref[0, 0, number]
        mine[2 * slots :, :] = jnp.full((1, mine.shape[1]), count_ref[0, 0, number], jnp.int32)


def load_kernel(batch, lists_ref, rows_ref, table, sent_ref, buffer, list_ref, list_sem, sems):
    copies = load_table(rows_ref, table, sems) + [fetch_list(lists_ref, 0, list_ref, list_sem)]
    for copy in copies:
        copy.start()
    for copy in copies:
        copy.wait()
    gather_rows(batch, list_ref, table, buffer, sent_ref)


def gather_kernel(batch, slots, tasks, meta_ref, lists_ref, table, *refs):
    outs, (buffer, *held, sems) = refs[: len(tasks)], refs[len(tasks) :]
    copies = [
        fetch_list(lists_ref, task_list(meta_ref, task, slots)[1], held[n], sems.at[n])
        for n, task in enumerate(tasks)
    ]
    for n, task in enumerate(tasks):
        pl.when(task < task_count(meta_ref))(copies[n].start)
    for n, task in enumerate(tasks):

        @pl.when(task < task_count(meta_ref))
        def _():
            copies[n].wait()
            gather_rows(batch, held[n], table, buffer, outs[n])


def batch_task(
    batch, live, is_own, number, arrive, kinds_ref, relations_ref, local, remote, rel_out, out_ref,
    left, right, weights, scale,
):
    size, width = left.shape
    halves = width // LANES
    sent = local.shape[0]
    rel_count = relations_ref.shape[0]
    inverse = 1.0 / (batch - 1)

    @pl.when(live)
    def _():
        kinds = kinds_ref[pl.ds(number, 1), :]
        full = relations_ref[...]
        high = full.astype(bf16)
        rest = full - high.astype(f32)
        middle = rest.astype(bf16)
        low = (rest - middle.astype(f32)).astype(bf16)
        kind_rows = lax.broadcasted_iota(jnp.int32, (rel_count, size), 0)
        onehot = jnp.where(kind_rows == kinds, 1.0, 0.0).astype(bf16)
        diagonal = lax.dot_general(
            jnp.concatenate([onehot, onehot, onehot], axis=0),
            jnp.concatenate([high, middle, low], axis=0),
            (((0,), (0,)), ((), ())),
            preferred_element_type=f32,
        )
        scale[...] = jnp.where(is_own, diagonal, 1.0)
        arrive()
        left[:sent, :] = (0.5 * (local[...].astype(f32) * scale[:sent, :]).astype(bf16).astype(f32)).astype(bf16)
        right[:sent, :] = (remote[...].astype(f32) * jnp.where(is_own, 1.0, diagonal[:sent, :])).astype(bf16)
        if size > sent:
            left[sent:, :] = jnp.zeros((size - sent, width), bf16)
            right[sent:, :] = jnp.zeros((size - sent, width), bf16)
        bends = jnp.tanh(
            lax.dot_general(left[...], right[...], (((1,), (1,)), ((), ())), preferred_element_type=f32)
        )
        weights[...] = (bends * (0.5 * inverse) + 0.5 * inverse).astype(bf16)
        side = LANES
        on_diag = lax.broadcasted_iota(jnp.int32, (side, side), 0) == lax.broadcasted_iota(
            jnp.int32, (side, side), 1
        )
        for start in range(0, size, side):
            probs = 0.5 * bends[start : start + side, start : start + side] + 0.5
            square = jnp.where(on_diag, probs - 1.0, probs * inverse).astype(bf16)
            weights[pl.ds(start, side), pl.ds(start, side)] = square
        grads = jnp.dot(weights[...], right[...], preferred_element_type=f32)
        scaled = grads * scale[...]
        for h in range(halves):
            out_ref[pl.ds(h, sent, stride=halves), :] = scaled[:sent, h * LANES : (h + 1) * LANES]
        terms = jnp.where(is_own, grads[:sent, :] * local[...].astype(f32), 0.0)
        terms_high = terms.astype(bf16)
        terms_low = (terms - terms_high.astype(f32)).astype(bf16)
        kind_part = onehot[:, :sent]
        rel_grad = (
            rel_out[...]
            + jnp.dot(kind_part, terms_high, preferred_element_type=f32)
            + jnp.dot(kind_part, terms_low, preferred_element_type=f32)
        )
        rel_out[...] = rel_grad


def pair_kernel(batch, slots, pair, pairs, meta_ref, kinds_ref, relations_ref, rel_in, *refs):
    mine, theirs, refs = refs[: 2 * pairs], refs[2 * pairs : 4 * pairs], refs[4 * pairs :]
    rel_out, out, left, right, weights, scale, local, remote, sems = refs
    rel_out[...] = rel_in[...]
    last = (task_count(meta_ref) - 1) >> 1 if pair is None else pair

    def copies(part, place):
        return [
            pltpu.make_async_copy(mine[2 * place + part], local.at[part], sems.at[part, 0]),
            pltpu.make_async_copy(theirs[2 * place + part], remote.at[part], sems.at[part, 1]),
        ]

    for part in range(2):
        for place in range(pairs):
            here = 2 * last + part < task_count(meta_ref)
            if pair is None:
                here = here & (last == place)

            @pl.when(here)
            def _():
                for copy in copies(part, place):
                    copy.start()

    def one_task(part, carry):
        task = 2 * last + part
        live = task < task_count(meta_ref)

        def arrive():
            pltpu.make_async_copy(mine[0], local.at[part], sems.at[part, 0]).wait()
            pltpu.make_async_copy(theirs[0], remote.at[part], sems.at[part, 1]).wait()

        is_own, number = task_list(meta_ref, task, slots)
        is_own = jnp.where(task < 2, task, jnp.where(is_own, 0, 1)) == 0
        number = jnp.where(task < 2, task * slots, number)
        batch_task(
            batch, live, is_own, number, arrive, kinds_ref, relations_ref, local.at[part], remote.at[part], rel_out,
            out.at[part], left, right, weights, scale,
        )
        return carry

    lax.fori_loop(0, 2, one_task, 0)


def nothing_kernel(*outs):
    pass


def add_grads(batch, halves, lives, numbers, lists_ref, grads, totals, held, sems):
    copies = [fetch_list(lists_ref, number, held[n], sems.at[n]) for n, number in enumerate(numbers)]
    for live, copy in zip(lives, copies):
        pl.when(live)(copy.start)
    for n, (live, copy) in enumerate(zip(lives, copies)):

        @pl.when(live)
        def _():
            copy.wait()
            scatter_rows(batch, halves, held[n], grads[n], totals)


def add_kernel(batch, slots, halves, pair, meta_ref, lists_ref, grads, *refs):
    totals, (own, sent, sems) = refs[-3 - SUMS : -3], refs[-3:]
    if pair == 0:
        for total in totals:
            total[...] = jnp.zeros_like(total)
    live = pair < (task_count(meta_ref) - 1) >> 1
    numbers = [task_list(meta_ref, 2 * pair + part, slots)[1] for part in range(2)]
    add_grads(batch, halves, (live, live), numbers, lists_ref, (grads.at[0], grads.at[1]), totals, (own, sent), sems)


def add_last_kernel(batch, slots, halves, meta_ref, lists_ref, grads, *refs):
    totals, (own, sent, sems) = refs[SUMS : 2 * SUMS], refs[2 * SUMS :]
    last = (task_count(meta_ref) - 1) >> 1
    tasks = [2 * last, 2 * last + 1]
    lives = [task < task_count(meta_ref) for task in tasks]
    numbers = [jnp.where(task < 2, task * slots, task_list(meta_ref, task, slots)[1]) for task in tasks]
    add_grads(batch, halves, lives, numbers, lists_ref, (grads.at[0], grads.at[1]), totals, (own, sent), sems)


def update_kernel(batch, more, state_ref, rows_ref, *refs):
    totals, refs = refs[:SUMS], refs[SUMS:]
    if more:
        lists_ref, new_state, new_rows, table, sent_ref, in_sems, out_sems, buffer, list_ref, list_sem = refs
        first_list = fetch_list(lists_ref, 0, list_ref, list_sem)
        first_list.start()
    else:
        new_state, new_rows, table, in_sems, out_sems = refs
    halves, count = table.shape[0], rows_ref.shape[0]
    width = halves * LANES
    chunk = LANES
    unroll = 16
    group = unroll * chunk

    def out_copies(number):
        rows = pl.ds(pl.multiple_of(number * group, group), group)
        return [
            pltpu.make_async_copy(
                table.at[h, rows, :], new_rows.at[rows, pl.ds(h * LANES, LANES)], out_sems.at[number, h]
            )
            for h in range(halves)
        ]

    def in_copies(number):
        rows = pl.ds(pl.multiple_of(number * group, group), group)
        return [
            pltpu.make_async_copy(
                rows_ref.at[rows, pl.ds(h * LANES, LANES)], table.at[h, rows, :], in_sems.at[number, h]
            )
            for h in range(halves)
        ]

    def begin(number, carry):
        for copy in in_copies(number):
            copy.start()
        return carry

    def update_group(number, carry):
        for copy in in_copies(number):
            copy.wait()
        for u in range(unroll):
            at = number * unroll + u
            first = pl.multiple_of(at * chunk, chunk)
            rows = pl.ds(first, chunk)
            grads = [
                sum(total[pl.ds(first * halves + h, chunk, stride=halves), :] for total in totals)
                for h in range(halves)
            ]
            squares = sum(g * g for g in grads)
            mean = jnp.sum(jnp.transpose(squares), axis=0, keepdims=True) * (1.0 / width)
            now = state_ref[pl.ds(at, 1), :] + mean
            new_state[pl.ds(at, 1), :] = now
            factor = jnp.transpose(jnp.broadcast_to(learn_rate * lax.rsqrt(now), (chunk, LANES)))
            for h in range(halves):
                table[h, rows, :] = table[h, rows, :] - grads[h] * factor
        for copy in out_copies(number):
            copy.start()
        return carry

    def finish(number, carry):
        for copy in out_copies(number):
            copy.wait()
        return carry

    lax.fori_loop(0, count // group, begin, 0)
    lax.fori_loop(0, count // group, update_group, 0)
    if more:
        first_list.wait()
        gather_rows(batch, list_ref, table, buffer, sent_ref)
    lax.fori_loop(0, count // group, finish, 0)


def update_relations(relations, rel_state, rel_total):
    rel_state = rel_state + rel_total * rel_total
    return relations - rel_rate * rel_total / jnp.sqrt(rel_state), rel_state


def params(mib):
    return pltpu.CompilerParams(vmem_limit_bytes=mib * MIB)


def in_vmem(array):
    return pltpu.with_memory_space_constraint(array, pltpu.VMEM)


def in_hbm(array):
    return pltpu.with_memory_space_constraint(array, pltpu.HBM)


def cost(us):
    return pl.CostEstimate(flops=0, bytes_accessed=int(us * 3.4e6), transcendentals=0)


def on_device(
    embeddings, row_state, relations, rel_state, edge_src, edge_dst, edge_rel, batch_count
):
    bit_count = lax.axis_size("dom").bit_length() - 1
    row_count, width = embeddings.shape
    slots, batch = edge_src.shape[3:]
    halves = width // LANES
    size = -(-batch // 256) * 256
    sent_size = -(-batch // 16) * 16
    list_size = -(-batch // 1024) * 1024
    pairs = slots
    sent_shape = jax.ShapeDtypeStruct((sent_size, width), bf16)
    grads_shape = jax.ShapeDtypeStruct((halves * sent_size + SPARE, LANES), f32)
    rel_shape = jax.ShapeDtypeStruct(relations.shape, f32)
    table_shape = pltpu.VMEM((halves, row_count + SPARE, LANES), f32)
    total_shape = pltpu.VMEM((halves * row_count + SPARE, LANES), f32)
    buffer = pltpu.VMEM((halves, sent_size + SPARE, LANES), f32)
    one_list = pltpu.SMEM((list_size,), jnp.int32)
    dma = pltpu.SemaphoreType.DMA
    task_scratch = [
        pltpu.VMEM((size, width), bf16),
        pltpu.VMEM((size, width), bf16),
        pltpu.VMEM((size, size), bf16),
        pltpu.VMEM((size, width), f32),
    ]
    swaps = [1 << (bit_count - 1 - number) for number in range(ROUNDS)]

    state = row_state.reshape(row_count // LANES, LANES)
    list_shape = jax.ShapeDtypeStruct((slots, list_size), jnp.int32)
    prepared = pl.pallas_call(
        prepare_kernel,
        out_shape=[list_shape] * ROUNDS + [jax.ShapeDtypeStruct((2 * slots + 1, list_size), jnp.int32)] * ROUNDS,
        in_specs=[VMEM_SPEC] * 3 + [SMEM_SPEC],
        out_specs=[VMEM_SPEC] * (2 * ROUNDS),
        compiler_params=params(16),
        cost_estimate=cost(1),
        name="prepare",
    )(in_hbm(edge_src), in_hbm(edge_dst), in_hbm(edge_rel), batch_count)
    sources, mine = prepared[:ROUNDS], prepared[ROUNDS:]
    theirs = [from_partner(mine[number], "dom", swaps[number]) for number in range(ROUNDS)]
    is_low = jnp.stack([(lax.axis_index("dom") & swap == 0).astype(jnp.int32) for swap in swaps])
    is_low, sources = lax.optimization_barrier((is_low, sources))
    table, sent = pl.pallas_call(
        functools.partial(load_kernel, batch),
        out_shape=[table_shape, sent_shape],
        in_specs=[ANY_SPEC, HBM_SPEC],
        out_specs=[VMEM_SPEC] * 2,
        scratch_shapes=[buffer, one_list, dma, dma((halves,))],
        compiler_params=params(16),
        cost_estimate=cost(5),
        name="load_and_gather",
    )(sources[0].reshape(-1), in_hbm(embeddings))
    got_a = from_partner(sent, "dom", swaps[0])

    rounds = []
    for number in range(ROUNDS):
        count = batch_count[0, :, number]
        their = theirs[number]
        lists = jnp.concatenate([sources[number], their[:slots]], axis=0).reshape(-1)
        kinds = jnp.concatenate([edge_rel[0, 0, number], their[slots : 2 * slots, :batch]], axis=0)
        kinds = jnp.pad(kinds, ((0, 0), (0, size - batch)), constant_values=-1)
        rounds.append((lists, kinds, jnp.concatenate([count, their[2 * slots, :1], is_low[number : number + 1]])))
    rounds = lax.optimization_barrier(rounds)

    for number in range(ROUNDS):
        swap = swaps[number]
        lists, kinds, meta = rounds[number]

        def gather(tasks, us, table):
            return pl.pallas_call(
                functools.partial(gather_kernel, batch, slots, tasks),
                out_shape=[sent_shape] * len(tasks),
                in_specs=[SMEM_SPEC, ANY_SPEC, VMEM_SPEC],
                out_specs=[VMEM_SPEC] * len(tasks),
                scratch_shapes=[buffer] + [one_list] * len(tasks) + [dma((len(tasks),))],
                compiler_params=params(16),
                cost_estimate=cost(us / 8),
                name="gather",
            )(meta, lists, in_vmem(table))

        if number > 0:
            got_a = from_partner(sent, "dom", swap)
        (second,) = gather((1,), 2, table)
        got_b = from_partner(second, "dom", swap)
        if number == 0:
            table, got_a = lax.optimization_barrier((table, got_a))
        sent = [sent, second, *gather(tuple(range(2, 2 * slots)), 6, table)]
        if number > 0:
            rel_total, sent = lax.optimization_barrier((rel_total, sent))
            rel_total = rel_total + from_partner(rel_total, *sums[-1])
            relations, rel_state = update_relations(relations, rel_state, rel_total)
        late, sent, got_b = lax.optimization_barrier((meta, sent, got_b))
        tasks = late[0] + late[1]
        got_a, got_b = got_b, got_a

        both_grads = jax.ShapeDtypeStruct((2, *grads_shape.shape), f32)

        def run_pair(pair, relations, sent, got, rel_grad):
            return pl.pallas_call(
                functools.partial(pair_kernel, batch, slots, pair, len(sent) // 2),
                out_shape=[rel_shape, both_grads],
                in_specs=[SMEM_SPEC] + [VMEM_SPEC] * 3 + [ANY_SPEC] * (2 * len(sent)),
                out_specs=[VMEM_SPEC] * 2,
                scratch_shapes=task_scratch + [pltpu.VMEM((2, *sent_shape.shape), bf16)] * 2 + [dma((2, 2))],
                compiler_params=params(16),
                cost_estimate=cost(6),
                name="batches",
            )(meta, kinds, relations, rel_grad, *sent, *got)

        def nothing(*shapes):
            return pl.pallas_call(
                nothing_kernel, out_shape=list(shapes), out_specs=[ANY_SPEC] * len(shapes), name="nothing"
            )()

        rel_grad = jnp.zeros(relations.shape, f32)
        grads, got = [], [got_a, got_b]
        for pair in range(pairs - 1):

            def go_on(tasks, relations, sent, got, rel_grad):
                next_a = from_partner(sent[2], "dom", swap)
                rel_grad, grads = run_pair(pair, relations, sent[:2], got, rel_grad)
                second, rel_grad = lax.optimization_barrier((sent[3], rel_grad))
                next_b = lax.cond(
                    tasks > 2 * pair + 3,
                    lambda second: from_partner(second, "dom", swap),
                    lambda second: nothing(sent_shape)[0],
                    second,
                )
                return next_a, next_b, rel_grad, grads

            def skip(tasks, relations, sent, got, rel_grad):
                next_a, next_b, grads = nothing(sent_shape, sent_shape, both_grads)
                return next_a, next_b, rel_grad, grads

            *next_got, rel_grad, part = lax.cond(
                tasks > 2 * pair + 2, go_on, skip, tasks, relations, sent[2 * pair : 2 * pair + 4], got[-2:], rel_grad
            )
            got += next_got
            grads.append(part)
        rel_grad, last_grads = run_pair(None, relations, sent, got, rel_grad)
        grads.append(last_grads)

        sums = [("dom", 1 << bit) for bit in reversed(range(bit_count))]
        sums += [("rep", 1 << bit) for bit in reversed(range(lax.axis_size("rep").bit_length() - 1))]
        rel_total, totals = rel_grad, None
        for step in range(max(pairs, len(sums))):
            part = from_partner(rel_total, *sums[step]) if step < len(sums) - (number + 1 < ROUNDS) else None
            if step < pairs:
                last = step == pairs - 1
                totals = pl.pallas_call(
                    functools.partial(add_last_kernel, batch, slots, halves)
                    if last
                    else functools.partial(add_kernel, batch, slots, halves, step),
                    out_shape=[total_shape] * SUMS,
                    in_specs=[SMEM_SPEC, ANY_SPEC] + [VMEM_SPEC] * (1 + SUMS * (step > 0)),
                    out_specs=[VMEM_SPEC] * SUMS,
                    scratch_shapes=[one_list, one_list, dma((2,))],
                    input_output_aliases={3 + n: n for n in range(SUMS)} if step > 0 else {},
                    compiler_params=params(12),
                    cost_estimate=cost(4),
                    name="add_rows",
                )(meta, lists, grads[step], *(map(in_vmem, totals) if step > 0 else []))
            if part is not None:
                rel_total = rel_total + part
            if step < pairs:
                rel_total, totals = lax.optimization_barrier((rel_total, totals))
        more = number + 1 < ROUNDS
        state, embeddings, *tables = pl.pallas_call(
            functools.partial(update_kernel, batch, more),
            out_shape=[jax.ShapeDtypeStruct(state.shape, f32), pltpu.HBM(embeddings.shape, f32)]
            + [table_shape, sent_shape] * more,
            in_specs=[VMEM_SPEC, HBM_SPEC] + [VMEM_SPEC] * SUMS + [ANY_SPEC] * more,
            out_specs=[VMEM_SPEC, HBM_SPEC] + [VMEM_SPEC] * (2 * more),
            scratch_shapes=[table_shape] * (not more) + [dma((row_count // (16 * LANES), halves))] * 2
            + [buffer, one_list, dma] * more,
            compiler_params=params(12),
            cost_estimate=cost(8),
            name="update",
        )(state, in_hbm(embeddings), *map(in_vmem, totals), *([rounds[number + 1][0]] if more else []))
        table, sent = tables if more else (None, None)
        if not more:
            relations, rel_state = update_relations(relations, rel_state, rel_total)
    return (embeddings, state.reshape(row_count), relations, rel_state)


def solution(mesh):
    return jax.shard_map(
        on_device,
        mesh=mesh,
        in_specs=(
            P(("dom", "rep"), None),
            P(("dom", "rep")),
            P(),
            P(),
            P("dom", "rep", None, None, None),
            P("dom", "rep", None, None, None),
            P("dom", "rep", None, None, None),
            P("dom", "rep", None),
        ),
        out_specs=(P(("dom", "rep"), None), P(("dom", "rep")), P(), P()),
        check_vma=False,
    )
```
